512 devices in a mesh: owner: 64 (over z, y), local: 8 (over x, core).
Axes of the slice: x: 4, y: 4, z: 16, core: 2. Of those that a mesh axis runs over, the one named last changes fastest.
Arguments:
- vectors: bfloat16 [8, 1048576], P(None, ('owner', 'local')), may hold values from -6 to 6
- leaf_basis: bfloat16 [64, 1048576], P(None, ('owner', 'local')), may hold values from -0.75 to 0.75
- near_blocks: bfloat16 [4, 64, 1048576], P(None, None, ('owner', 'local')), may hold values from -0.375 to 0.375
- near_source: int32 [16384, 4], P(('owner', 'local')), may hold values from 0 to 16383, as said below
- up_transfer: bfloat16 [64, 1048576], P(None, ('owner', 'local')), may hold values from -0.375 to 0.375
- far_owner: int32 [4096, 8], P(('owner', 'local')), may hold values from 0 to 63, all different within a row; in each aligned block of 8 rows (0 to 7, 8 to 15, ...) at most 2 rows name the same one
- far_member: int32 [4096, 8], P(('owner', 'local')), may hold values from 0 to 63
- far_count: int32 [4096], P(('owner', 'local')), may hold values from 4 to 8
- far_blocks: bfloat16 [8, 64, 262144], P(None, None, ('owner', 'local')), may hold values from -0.25 to 0.25
- root_transfer: bfloat16 [64, 262144], P(None, ('owner', 'local')), may hold values from -0.26367188 to 0.26367188
- top_source: int32 [64, 16], P('owner', 'local'), may hold values from 0 to 63, all different within a row
- top_blocks: bfloat16 [16, 64, 4096], P('local', None, 'owner'), may hold values from -0.1875 to 0.1875
Outputs:
- product: bfloat16 [8, 1048576], P(None, ('owner', 'local'))
The draws below stay inside these ranges and needn't reach their ends.
Inputs may be any that keep to these rules, and one draw needn't show every extreme that they name: `near_source`: slot 0 of each leaf's row is the leaf itself; every other slot names a leaf at most 4 leaves away from it. `far_owner`: each cluster's row names 8 different owners; among the 8 rows of one device no owner is named more than 2 times, a bound that some block reaches. `top_source`: each row names 16 different owners; every owner is named in some row.
All inputs are finite; a program needn't handle non-finite values.
Results may differ from the reference program's by a relative error of at most 0.009.
Values may be sent and summed in bfloat16 or wider, within the bound.
A program may use at most 64 MiB of HBM per device.

```python
import math
import jax
import jax.numpy as jnp
import numpy as np
from jax import lax

NV = 8
LEAF = 64
RANK = 64
CLUSTER_LEAVES = 4
NEAR = 4
REACH = 4
FAR = 8
C_DEV = 8
C_OWN = 64
CAP = 2
TOPN = 16
LEAVES = 16384
CLUSTERS = 4096
POINTS = 1048576
N_OWNER = 64


def draw_near_source(key, part):
    key = jax.random.fold_in(key, 11)
    keys = jax.random.split(key, LEAVES)
    offsets = jnp.concatenate([-jnp.arange(1, REACH + 1, dtype=jnp.int32), jnp.arange(1, REACH + 1, dtype=jnp.int32)])

    def choose(leaf_key):
        return jax.random.permutation(leaf_key, offsets)[:NEAR - 1]
    chosen = jax.vmap(choose)(keys)
    home = jnp.arange(LEAVES, dtype=jnp.int32)[:, None]
    moved = home + chosen
    inside = jnp.where((moved < 0) | (moved >= LEAVES), home - chosen, moved)
    return jnp.concatenate([home, inside], axis=1).astype(jnp.int32)


def with_ends(values, own_key, smallest, largest):
    shape = values.shape
    spot = [jax.random.randint(jax.random.fold_in(own_key, axis), (), 0, shape[axis]) for axis in range(len(shape))]
    values = values.at[tuple(spot)].set(smallest)
    longest = shape.index(max(shape))
    spot[longest] = (spot[longest] + 1) % shape[longest]
    return values.at[tuple(spot)].set(largest)


def shard_levels(key, dims, pieces, low, top_value):
    gain, own = 1.0, jax.random.fold_in(key, 6)
    for position, shards_of in pieces:
        heights = jnp.exp(jax.random.uniform(jax.random.fold_in(own, position), (shards_of,), jnp.float32, low / len(pieces), top_value / len(pieces)))
        gain = gain * jnp.repeat(heights, dims[position] // shards_of).reshape([-1 if axis == position else 1 for axis in range(len(dims))])
    return gain


def picks_of(own_key, rows, number_of, top, lift):
    order = jax.random.permutation(jax.random.fold_in(own_key, 1), number_of)
    favour = order
    for power in range(3):
        favour = favour * favour // number_of
    favour = favour * lift // number_of
    lots = jax.random.randint(jax.random.fold_in(own_key, 2), (rows, number_of), 0, 4096) + favour
    sure = jax.random.permutation(jax.random.fold_in(own_key, 3), rows)[jnp.arange(number_of) % rows]
    lots = jnp.where(jnp.arange(rows)[:, None] == sure[None, :], 1 << 14, lots)
    priority = lots * number_of + jnp.arange(number_of)
    return lax.top_k(priority.astype(jnp.int32), top)[1].astype(jnp.int32)


def routed_block(rng, own, number, rows, amount, top, most, skew):
    sequence = jax.random.permutation(rng, amount)
    packed, ordinary = load_shares(amount, rows * top, most, skew, True), load_shares(amount, rows * top, most, skew, False)
    places = jnp.arange(amount)

    def named(sizes, rotation):
        used = int((sizes > 0).sum())
        fixed = max(1, used // 4)
        passed = fixed + (places - fixed + rotation * (used - fixed)) % max(1, amount - fixed)
        return jnp.zeros((amount,), jnp.int32).at[sequence[jnp.where(places < fixed, places, passed)]].set(jnp.asarray(sizes, jnp.int32))

    sizes = jnp.where(number % 4 == 0, named(packed, number // 4), named(ordinary, number - number // 4 - 1))
    mixed = jax.random.permutation(jax.random.fold_in(own, 3), amount)
    source_of, sink = mixed[0:amount // 2 * 2:2], mixed[1:amount // 2 * 2:2]
    margin = jnp.minimum(sizes[source_of] - 1, most - sizes[sink]) // 2
    margin = jnp.where((source_of == sequence[0]) | (sink == sequence[0]) | (sizes[sink] == 0), 0, jnp.maximum(margin, 0))
    passed = jax.random.randint(jax.random.fold_in(own, 4), (amount // 2,), 0, 1 << 20) % (margin + 1)
    sizes = sizes.at[source_of].add(-passed).at[sink].add(passed)
    items = jnp.searchsorted(jnp.cumsum(sizes), jnp.arange(rows * top), side="right").astype(jnp.int32)
    grid = items.reshape(top, rows).T
    grid = grid[jax.random.permutation(jax.random.fold_in(own, 1), rows)]
    rotation = jax.random.randint(jax.random.fold_in(own, 2), (rows, 1), 0, top)
    return jnp.take_along_axis(grid, (jnp.arange(top)[None, :] + rotation) % top, axis=1)


def load_shares(number_of, total, reach, lean, full):
    loads = [(1 << 20) // math.isqrt(standing ** lean) + 1 for standing in range(1, number_of + 1)]
    largest = reach if full else min(reach, max(-(-total // number_of), total * loads[0] // sum(loads)))
    least = 1 if total - largest >= number_of - 1 else 0
    given, rest = [largest] + [least] * (number_of - 1), total - largest - least * (number_of - 1)
    while rest > 0:
        free = [i for i in range(1, number_of) if given[i] < largest] or [i for i in range(1, number_of) if given[i] < reach]
        whole, left = sum([loads[i] for i in free]), rest
        for i in free:
            addition = min(reach - given[i], max(1, left * loads[i] // whole), rest)
            given[i] = given[i] + addition
            rest = rest - addition
    return np.array(given)


def gaussian(stream_key, shape, scale, bound, cuts=(), kind=jnp.bfloat16):
    drawn = jax.random.normal(stream_key, shape, jnp.float32) * scale
    if len(cuts) > 0:
        drawn = shard_levels(stream_key, shape, cuts, -0.22, 0.18) * drawn
    return jnp.clip(drawn, min=-bound, max=bound).astype(kind)


def setup_inputs(seed: int = 0) -> dict:
    splits = jax.random.split(jax.random.key(seed), 13)
    vectors = gaussian(splits[0], (NV, POINTS), 1.0, 6.0, ((1, 512),))
    leaf_basis = gaussian(splits[1], (RANK, POINTS), LEAF ** -0.5, 0.75, ((1, 512),))
    near_blocks = gaussian(splits[2], (NEAR, LEAF, POINTS), (NEAR * LEAF) ** -0.5, 0.375, ((2, 512),))
    near_source = draw_near_source(jax.random.fold_in(splits[12], 71), 0)
    up_transfer = gaussian(splits[4], (RANK, LEAVES * RANK), (CLUSTER_LEAVES * RANK) ** -0.5, 0.375, ((1, 512),))
    far_owner_keys = jax.random.split(jax.random.fold_in(splits[5], 1), CLUSTERS // C_DEV)
    far_owner_turns = jax.random.permutation(jax.random.fold_in(splits[5], 3), CLUSTERS // C_DEV)
    far_owner = jax.vmap(lambda own, number: routed_block(jax.random.fold_in(splits[5], 2), own, number, C_DEV, N_OWNER, FAR, CAP, 2))(far_owner_keys, far_owner_turns).reshape((CLUSTERS, FAR))
    far_member = with_ends(jax.random.randint(splits[6], (CLUSTERS, FAR), 0, C_OWN), jax.random.fold_in(splits[6], 1), 0, C_OWN - 1).astype(jnp.int32)
    far_count = with_ends(jax.random.randint(splits[7], (CLUSTERS,), FAR // 2, FAR + 1), jax.random.fold_in(splits[7], 1), FAR // 2, FAR).astype(jnp.int32)
    far_blocks = gaussian(splits[8], (FAR, RANK, CLUSTERS * RANK), (FAR * RANK) ** -0.5, 0.25, ((2, 512),))
    root_transfer = gaussian(splits[9], (RANK, CLUSTERS * RANK), ((RANK * RANK * C_OWN) ** -0.25), 0.26367188, ((1, 512),))
    top_source = picks_of(splits[10], N_OWNER, N_OWNER, TOPN, 0)
    top_blocks = gaussian(splits[11], (TOPN, RANK, N_OWNER * RANK), (TOPN * RANK) ** -0.5, 0.1875, ((0, 8), (2, 64)))
    return dict(vectors=vectors, leaf_basis=leaf_basis, near_blocks=near_blocks, near_source=near_source, up_transfer=up_transfer, far_owner=far_owner, far_member=far_member, far_count=far_count, far_blocks=far_blocks, root_transfer=root_transfer, top_source=top_source, top_blocks=top_blocks)


def rounded(value):
    return lax.optimization_barrier(value.astype(jnp.bfloat16)).astype(jnp.float32)


def reference(vectors, leaf_basis, near_blocks, near_source, up_transfer, far_owner, far_member, far_count, far_blocks, root_transfer, top_source, top_blocks):
    leaf_total = leaf_basis.shape[1] // LEAF
    cluster_total = leaf_total // CLUSTER_LEAVES
    owner_total = cluster_total // C_OWN
    points = vectors.reshape(NV, leaf_total, LEAF).astype(jnp.float32)
    basis = leaf_basis.reshape(RANK, leaf_total, LEAF).astype(jnp.float32)
    leaf_skel = rounded(jnp.einsum("vlp,klp->lvk", points, basis))
    upward = up_transfer.reshape(RANK, cluster_total, CLUSTER_LEAVES, RANK).astype(jnp.float32)
    cluster_skel = rounded(jnp.einsum("tcvk,jtck->tvj", leaf_skel.reshape(cluster_total, CLUSTER_LEAVES, NV, RANK), upward))
    sources = far_owner * C_OWN + far_member
    picked = cluster_skel[sources]
    live = (jnp.arange(FAR, dtype=jnp.int32)[None, :] < far_count[:, None]).astype(jnp.float32)
    picked = picked * live[:, :, None, None]
    couplings = far_blocks.reshape(FAR, RANK, cluster_total, RANK).astype(jnp.float32)
    far_field = jnp.einsum("tfvk,fjtk->tvj", picked, couplings)
    rootward = root_transfer.reshape(RANK, owner_total, C_OWN, RANK).astype(jnp.float32)
    root_skel = rounded(jnp.einsum("ocvk,jock->ovj", cluster_skel.reshape(owner_total, C_OWN, NV, RANK), rootward))
    top_float = top_blocks.reshape(TOPN, RANK, owner_total, RANK).astype(jnp.float32)
    coupled = root_skel[top_source]
    root_out = rounded(jnp.einsum("osvk,sjok->ovj", coupled, top_float))
    downward = jnp.einsum("ovj,jock->ocvk", root_out, rootward).reshape(cluster_total, NV, RANK)
    cluster_out = rounded(far_field + downward)
    leaf_out = rounded(jnp.einsum("tvj,jtck->tcvk", cluster_out, upward).reshape(leaf_total, NV, RANK))
    result = jnp.einsum("lvk,klp->vlp", leaf_out, basis)
    for slot_index in range(NEAR):
        gathered = points[:, near_source[:, slot_index], :]
        dense = near_blocks[slot_index].reshape(LEAF, leaf_total, LEAF).astype(jnp.float32)
        result = result + jnp.einsum("vlp,qlp->vlq", gathered, dense)
    return result.reshape(NV, leaf_total * LEAF).astype(jnp.bfloat16)
```

```python
import functools

import jax
import jax.numpy as jnp
from jax import lax
from jax.experimental import pallas as pl
from jax.experimental.pallas import tpu as pltpu
from jax.sharding import PartitionSpec as P

MESH = pl.DeviceIdType.MESH
NV = 8
LEAF = 64
RANK = 64
CLUSTER_LEAVES = 4
REACH = 4
HALF = 64
WIDE = 128
QUAD = 256


def dot(left, right):
    return jnp.dot(left, right, preferred_element_type=jnp.float32)


def dot_t(left, right):
    return lax.dot_general(left, right, (((1,), (1,)), ((), ())), preferred_element_type=jnp.float32)


def wait_bytes(ref, sem):
    pltpu.make_async_copy(ref, ref, sem).wait()


def kernel(
    owners,
    locals_,
    vec,
    basis,
    near,
    up,
    far,
    root_t,
    top_b,
    near_src,
    owner_s,
    count_s,
    owner_v,
    member_v,
    top_src,
    out,
    vec_b,
    basis_b,
    near_b,
    up_b,
    far_b,
    root_b,
    topb_b,
    load_sem,
    pair_basis,
    ext,
    near_res,
    rank_b,
    rank_s,
    halo,
    req_row,
    req,
    req_s,
    tops_row,
    tops,
    tops_s,
    topw,
    skel,
    part,
    root_tile,
    roots,
    far_send,
    far_recv,
    share,
    smem_sem,
    send_sem,
    recv_sem,
):
    o, l = lax.axis_index("owner"), lax.axis_index("local")
    me = o * locals_ + l
    total = owners * locals_
    clusters = skel.shape[0] // locals_
    slots = far_b.shape[0]
    near_slots = near_b.shape[0]
    leaves = clusters * CLUSTER_LEAVES
    pairs = leaves // 2
    rounds = owners // locals_
    left, right = lax.rem(me + total - 1, total), lax.rem(me + 1, total)
    left_id = (left // locals_, lax.rem(left, locals_))
    right_id = (right // locals_, lax.rem(right, locals_))
    HALO, REQ, TOPS, TOPW, SKEL, PART, ROOT, FARS, SHARE, HALO2 = range(10)

    def load(i, source, target):
        copy = pltpu.make_async_copy(source, target, load_sem.at[i])
        copy.start()
        return copy

    load_vec = load(0, vec, vec_b)
    load_basis = load(1, basis, basis_b)
    load_up = load(2, up, up_b)
    load_root = load(3, root_t, root_b)
    load_topb = load(4, top_b, topb_b)
    load_near = load(5, near, near_b)
    load_far = load(6, far, far_b)

    def remote(source, target, kind, device):
        return pltpu.make_async_remote_copy(
            src_ref=source,
            dst_ref=target,
            send_sem=send_sem.at[kind],
            recv_sem=recv_sem.at[kind],
            device_id=device,
            device_id_type=MESH,
        )

    barrier = pltpu.get_barrier_semaphore()

    def greet(device):
        pl.semaphore_signal(barrier, inc=1, device_id=device, device_id_type=MESH)

    @pl.loop(1, locals_)
    def _(d):
        greet((o, lax.rem(l + d, locals_)))

    greet(left_id)
    greet(right_id)

    @pl.loop(1, owners)
    def _(d):
        greet((lax.rem(o + d, owners), l))

    lane = lax.broadcasted_iota(jnp.int32, (1, WIDE), 1)
    lanes = lax.broadcasted_iota(jnp.int32, (clusters, WIDE), 1)
    key = jnp.where(lanes >= HALF, lanes - HALF, lanes)
    named = jnp.zeros((clusters, WIDE), jnp.int32)
    member = jnp.zeros((clusters, WIDE), jnp.int32)
    for f in range(slots):
        same = owner_v[:, f : f + 1] == key
        named = jnp.where(same, 1, named)
        member = jnp.where(same, member_v[:, f : f + 1], member)
    second = (lane >= HALF).astype(jnp.int32)
    run = jnp.zeros((1, WIDE), jnp.int32)
    wanted = jnp.zeros((1, WIDE), jnp.int32)
    for t in range(clusters):
        rank_b[t : t + 1, :] = run
        wanted = jnp.where(run == second, wanted + member[t : t + 1], wanted)
        run = run + named[t : t + 1]
    req_row[...] = wanted
    req[pl.ds(o, 1), :, :] = wanted.reshape(1, 1, WIDE)
    rank_copy = pltpu.make_async_copy(rank_b, rank_s, smem_sem.at[0])
    rank_copy.start()
    tops_row[...] = jnp.zeros((1, WIDE), jnp.int32)
    tops_row[:, 0:2] = top_src[...]
    tops[pl.ds(l, 1), :, :] = tops_row[...].reshape(1, 1, WIDE)

    low = lax.broadcasted_iota(jnp.int32, (NV, WIDE), 1) < HALF
    low_ones = (lax.broadcasted_iota(jnp.int32, (RANK, WIDE), 1) < HALF).astype(jnp.bfloat16)
    high_ones = (lax.broadcasted_iota(jnp.int32, (RANK, WIDE), 1) >= HALF).astype(jnp.bfloat16)
    load_vec.wait()
    load_basis.wait()
    load_up.wait()
    first = l * clusters
    tiles = []
    for t in range(clusters):
        parts = []
        for q in (2 * t, 2 * t + 1):
            block = basis_b[:, q * WIDE : (q + 1) * WIDE]
            diagonal = jnp.concatenate([block * low_ones, block * high_ones], axis=0)
            pair_basis[q] = diagonal
            parts.append(dot_t(vec_b[:, q * WIDE : (q + 1) * WIDE], diagonal))
        leaf_skel = jnp.concatenate(parts, axis=1).astype(jnp.bfloat16)
        block = up_b[:, t * QUAD : (t + 1) * QUAD]
        tile = dot_t(leaf_skel, jnp.concatenate([block, block], axis=0)).astype(jnp.bfloat16)
        skel[pl.ds(first + t, 1), :, :] = tile.reshape(1, NV, WIDE)
        tiles.append(tile.astype(jnp.float32))
    load_root.wait()
    rows = jnp.concatenate(
        [jnp.where(low, tiles[2 * q], tiles[2 * q + 1]) for q in range(clusters // 2)], axis=1
    ).astype(jnp.bfloat16)
    rootward = root_b[...]
    part[pl.ds(l, 1), :, :] = dot_t(rows, jnp.concatenate([rootward, rootward], axis=0)).reshape(1, NV, WIDE)

    load_topb.wait()
    topw[pl.ds(l, 1), :, :] = jnp.concatenate([topb_b[0], topb_b[1]], axis=1).reshape(1, RANK, WIDE)

    pl.semaphore_wait(barrier, owners - 1 + locals_ - 1 + 2)

    @pl.loop(1, locals_)
    def _(d):
        peer = (o, lax.rem(l + d, locals_))
        own = skel.at[pl.ds(first, clusters)]
        remote(own, own, SKEL, peer).start()
        mine = part.at[pl.ds(l, 1)]
        remote(mine, mine, PART, peer).start()

    @pl.loop(1, owners)
    def _(d):
        target = req.at[pl.ds(o, 1)]
        remote(target, target, REQ, (lax.rem(o + d, owners), l)).start()

    @pl.loop(1, locals_)
    def _(d):
        peer = (o, lax.rem(l + d, locals_))
        mine = tops.at[pl.ds(l, 1)]
        remote(mine, mine, TOPS, peer).start()
        block = topw.at[pl.ds(l, 1)]
        remote(block, block, TOPW, peer).start()

    edge = REACH * LEAF
    width = leaves * LEAF
    remote(vec_b.at[:, pl.ds(width - edge, edge)], halo.at[0], HALO, right_id).start()
    remote(vec_b.at[:, pl.ds(0, edge)], halo.at[1], HALO2, left_id).start()

    wait_bytes(part.at[pl.ds(0, locals_ - 1)], recv_sem.at[PART])
    root = part[0]
    for other in range(1, locals_):
        root = root + part[other]
    root_tile[...] = root.astype(jnp.bfloat16)

    @pl.when(l == 0)
    def _():
        roots[0] = root_tile[...]

    @pl.when(l != 0)
    def _():
        remote(root_tile, roots.at[0], ROOT, (lax.rem(o + l, owners), l)).start()

    @pl.loop(1, rounds)
    def _(i):
        remote(root_tile, roots.at[i], ROOT, (lax.rem(o + l + locals_ * i, owners), l)).start()

    wait_bytes(req.at[pl.ds(0, owners - 1)], recv_sem.at[REQ])
    req_copy = pltpu.make_async_copy(req, req_s, smem_sem.at[1])
    req_copy.start()
    wait_bytes(skel.at[pl.ds(0, clusters * (locals_ - 1))], recv_sem.at[SKEL])
    req_copy.wait()

    def chosen(asker):
        a = skel[req_s[asker, 0, o]].astype(jnp.float32)
        b = skel[req_s[asker, 0, HALF + o]].astype(jnp.float32)
        return jnp.where(low, a, b).astype(jnp.bfloat16).reshape(1, NV, WIDE)

    far_recv[pl.ds(o, 1), :, :] = chosen(o)

    @pl.loop(1, owners)
    def _(d):
        asker = lax.rem(o + d, owners)
        far_send[pl.ds(asker, 1), :, :] = chosen(asker)
        remote(far_send.at[pl.ds(asker, 1)], far_recv.at[pl.ds(o, 1)], FARS, (asker, l)).start()

    wait_bytes(tops.at[pl.ds(0, locals_ - 1)], recv_sem.at[TOPS])
    tops_copy = pltpu.make_async_copy(tops, tops_s, smem_sem.at[2])
    tops_copy.start()
    wait_bytes(topw.at[pl.ds(0, locals_ - 1)], recv_sem.at[TOPW])
    tops_copy.wait()

    @pl.when(l == 0)
    def _():
        wait_bytes(roots.at[pl.ds(0, rounds - 1)], recv_sem.at[ROOT])

    @pl.when(l != 0)
    def _():
        wait_bytes(roots, recv_sem.at[ROOT])

    def coupled(s):
        away = lax.rem(o - l - tops_s[s // 2, 0, s % 2] + 2 * owners, owners)
        tile = roots[away // locals_].astype(jnp.float32)
        return jnp.where(lax.rem(away, locals_) == 0, tile, 0.0)

    total_share = jnp.zeros((NV, WIDE), jnp.float32)
    for other in range(locals_):
        lhs = jnp.where(low, coupled(2 * other), coupled(2 * other + 1)).astype(jnp.bfloat16)
        block = topw[other]
        total_share = total_share + dot_t(lhs, jnp.concatenate([block, block], axis=0))
    share[pl.ds(l, 1), :, :] = total_share.reshape(1, NV, WIDE)

    @pl.loop(1, locals_)
    def _(d):
        mine = share.at[pl.ds(l, 1)]
        remote(mine, mine, SHARE, (o, lax.rem(l + d, locals_))).start()

    wait_bytes(halo.at[0], recv_sem.at[HALO])
    wait_bytes(halo.at[1], recv_sem.at[HALO2])

    def spread(pair, at):
        pair = pair.astype(jnp.float32)
        turned = pltpu.roll(pair, HALF, 1)
        ext[at] = jnp.where(low, pair, turned)
        ext[at + 1] = jnp.where(low, turned, pair)

    for q in range(REACH // 2):
        spread(halo[0, :, q * WIDE : (q + 1) * WIDE], 2 * q)
        spread(halo[1, :, q * WIDE : (q + 1) * WIDE], REACH + leaves + 2 * q)
    for q in range(pairs):
        spread(vec_b[:, q * WIDE : (q + 1) * WIDE], REACH + 2 * q)
    load_near.wait()
    zero = jnp.zeros((NV, WIDE), jnp.float32)

    def quad(pieces):
        rows = [
            jnp.concatenate([jnp.where(low, pieces[0], 0.0), zero], axis=1),
            jnp.concatenate([jnp.where(low, 0.0, pieces[1]), zero], axis=1),
            jnp.concatenate([zero, jnp.where(low, pieces[2], 0.0)], axis=1),
            jnp.concatenate([zero, jnp.where(low, 0.0, pieces[3])], axis=1),
        ]
        return jnp.concatenate(rows, axis=0).astype(jnp.bfloat16)

    offset = REACH - me * leaves

    def inside(at):
        return jnp.minimum(jnp.maximum(at, 0), leaves + 2 * REACH - 1)

    for t in range(clusters):
        acc = jnp.zeros((CLUSTER_LEAVES * NV, LEAF), jnp.float32)
        for i in range(near_slots):
            lhs = quad([ext[inside(near_src[i, CLUSTER_LEAVES * t + c] + offset)] for c in range(CLUSTER_LEAVES)])
            acc = acc + dot_t(lhs, near_b[i, :, t * QUAD : (t + 1) * QUAD])
        for c in range(0, CLUSTER_LEAVES, 2):
            near_res[2 * t + c // 2] = jnp.concatenate(
                [acc[c * NV : (c + 1) * NV], acc[(c + 1) * NV : (c + 2) * NV]], axis=1
            )

    wait_bytes(share.at[pl.ds(0, locals_ - 1)], recv_sem.at[SHARE])
    summed = share[0]
    for other in range(1, locals_):
        summed = summed + share[other]
    root_out = summed[:, 0:RANK].astype(jnp.bfloat16)
    downward = dot(root_out, root_b[...])
    rank_copy.wait()
    load_far.wait()

    wait_bytes(far_recv.at[pl.ds(0, owners - 1)], recv_sem.at[FARS])

    def picked(t, f):
        source = owner_s[t, f]
        tile = far_recv[source].astype(jnp.float32)
        tile = jnp.where(rank_s[t, source] == t % 2, tile, pltpu.roll(tile, HALF, 1))
        return jnp.where(f < count_s[t], tile, 0.0)

    for g in range(clusters // 4):
        acc = jnp.zeros((4 * NV, RANK), jnp.float32)
        for f in range(slots):
            lhs = quad([picked(4 * g + t, f) for t in range(4)])
            acc = acc + dot_t(lhs, far_b[f, :, g * QUAD : (g + 1) * QUAD])
        for t in range(4):
            at = 4 * g + t
            cluster_out = acc[t * NV : (t + 1) * NV] + downward[:, at * RANK : (at + 1) * RANK]
            leaf_out = dot(cluster_out.astype(jnp.bfloat16), up_b[:, at * QUAD : (at + 1) * QUAD]).astype(jnp.bfloat16)
            for c in range(2):
                q = 2 * at + c
                result = dot(leaf_out[:, c * WIDE : (c + 1) * WIDE], pair_basis[q]) + near_res[q]
                out[:, q * WIDE : (q + 1) * WIDE] = result.astype(jnp.bfloat16)

    wait_bytes(skel.at[pl.ds(0, clusters * (locals_ - 1))], send_sem.at[SKEL])
    wait_bytes(part.at[pl.ds(0, locals_ - 1)], send_sem.at[PART])
    wait_bytes(req.at[pl.ds(0, owners - 1)], send_sem.at[REQ])
    wait_bytes(tops.at[pl.ds(0, locals_ - 1)], send_sem.at[TOPS])
    wait_bytes(topw.at[pl.ds(0, locals_ - 1)], send_sem.at[TOPW])
    wait_bytes(halo.at[0], send_sem.at[HALO])
    wait_bytes(halo.at[1], send_sem.at[HALO2])

    @pl.when(l == 0)
    def _():
        wait_bytes(roots.at[pl.ds(0, rounds - 1)], send_sem.at[ROOT])

    @pl.when(l != 0)
    def _():
        wait_bytes(roots, send_sem.at[ROOT])

    wait_bytes(share.at[pl.ds(0, locals_ - 1)], send_sem.at[SHARE])
    wait_bytes(far_recv.at[pl.ds(0, owners - 1)], send_sem.at[FARS])


def per_device(
    owners,
    locals_,
    vectors,
    leaf_basis,
    near_blocks,
    near_source,
    up_transfer,
    far_owner,
    far_member,
    far_count,
    far_blocks,
    root_transfer,
    top_source,
    top_blocks,
):
    clusters = far_owner.shape[0]
    leaves = clusters * CLUSTER_LEAVES
    bf16, f32, i32 = jnp.bfloat16, jnp.float32, jnp.int32
    hbm = pl.BlockSpec(memory_space=pl.ANY)
    smem = pl.BlockSpec(memory_space=pltpu.SMEM)
    vmem = pl.BlockSpec(memory_space=pltpu.VMEM)
    big = (vectors, leaf_basis, near_blocks, up_transfer, far_blocks, root_transfer, top_blocks)
    return pl.pallas_call(
        functools.partial(kernel, owners, locals_),
        out_shape=jax.ShapeDtypeStruct(vectors.shape, bf16),
        in_specs=[hbm] * 7 + [smem] * 3 + [vmem] * 3,
        out_specs=vmem,
        scratch_shapes=[pltpu.VMEM(a.shape, bf16) for a in big]
        + [
            pltpu.SemaphoreType.DMA((7,)),
            pltpu.VMEM((leaves // 2, WIDE, WIDE), bf16),
            pltpu.VMEM((leaves + 2 * REACH, NV, WIDE), f32),
            pltpu.VMEM((leaves // 2, NV, WIDE), f32),
            pltpu.VMEM((clusters, WIDE), i32),
            pltpu.SMEM((clusters, WIDE), i32),
            pltpu.VMEM((2, NV, REACH * LEAF), bf16),
            pltpu.VMEM((1, WIDE), i32),
            pltpu.VMEM((owners, 1, WIDE), i32),
            pltpu.SMEM((owners, 1, WIDE), i32),
            pltpu.VMEM((1, WIDE), i32),
            pltpu.VMEM((locals_, 1, WIDE), i32),
            pltpu.SMEM((locals_, 1, WIDE), i32),
            pltpu.VMEM((locals_, RANK, WIDE), bf16),
            pltpu.VMEM((clusters * locals_, NV, WIDE), bf16),
            pltpu.VMEM((locals_, NV, WIDE), f32),
            pltpu.VMEM((NV, WIDE), bf16),
            pltpu.VMEM((owners // locals_, NV, WIDE), bf16),
            pltpu.VMEM((owners, NV, WIDE), bf16),
            pltpu.VMEM((owners, NV, WIDE), bf16),
            pltpu.VMEM((locals_, NV, WIDE), f32),
            pltpu.SemaphoreType.DMA((3,)),
            pltpu.SemaphoreType.DMA((10,)),
            pltpu.SemaphoreType.DMA((10,)),
        ],
        compiler_params=pltpu.CompilerParams(
            collective_id=0, has_side_effects=True, vmem_limit_bytes=32 * 1024 * 1024
        ),
    )(*big, near_source.T, far_owner, far_count, far_owner, far_member, top_source)


def solution(mesh):
    return jax.shard_map(
        functools.partial(per_device, mesh.shape["owner"], mesh.shape["local"]),
        mesh=mesh,
        in_specs=(
            P(None, ("owner", "local")),
            P(None, ("owner", "local")),
            P(None, None, ("owner", "local")),
            P(("owner", "local"), None),
            P(None, ("owner", "local")),
            P(("owner", "local"), None),
            P(("owner", "local"), None),
            P(("owner", "local")),
            P(None, None, ("owner", "local")),
            P(None, ("owner", "local")),
            P("owner", "local"),
            P("local", None, "owner"),
        ),
        out_specs=P(None, ("owner", "local")),
        check_vma=False,
    )
```

```python
import functools

import jax
import jax.numpy as jnp
from jax import lax
from jax.experimental import pallas as pl
from jax.experimental.pallas import tpu as pltpu
from jax.sharding import PartitionSpec as P

MESH = pl.DeviceIdType.MESH
KINDS = 13
NV = 8
LEAF = 64
RANK = 64
CLUSTER_LEAVES = 4
REACH = 4
HALF = 64
PLANE = 4
WIDE = 128
QUAD = 256


def dot(left, right):
    return jnp.dot(left, right, preferred_element_type=jnp.float32)


def dot_t(left, right):
    return lax.dot_general(left, right, (((1,), (1,)), ((), ())), preferred_element_type=jnp.float32)


def wait_bytes(ref, sem):
    pltpu.make_async_copy(ref, ref, sem).wait()


def kernel(
    owners,
    locals_,
    vec,
    basis,
    near,
    up,
    far,
    root_t,
    top_b,
    near_src_h,
    owner_h,
    member_h,
    count_h,
    top_src_h,
    out,
    vec_b,
    basis_b,
    near_b,
    up_b,
    far_b,
    root_b,
    topb_b,
    near_src,
    owner_s,
    count_s,
    owner_v,
    member_v,
    top_src,
    load_sem,
    pair_basis,
    ext,
    near_res,
    rank_b,
    rank_s,
    halo,
    req,
    req_s,
    tops_row,
    tops,
    tops_s,
    topw,
    skel,
    part,
    root_tile,
    roots,
    far_send,
    far_recv,
    share,
    smem_sem,
    send_sem,
    recv_sem,
    known,
):
    o, l = lax.axis_index("owner"), lax.axis_index("local")
    me = o * locals_ + l
    total = owners * locals_
    clusters = skel.shape[0] // locals_
    slots = far_b.shape[0]
    near_slots = near_b.shape[0]
    leaves = clusters * CLUSTER_LEAVES
    pairs = leaves // 2
    rounds = owners // locals_
    left, right = lax.rem(me + total - 1, total), lax.rem(me + 1, total)
    left_id = (left // locals_, lax.rem(left, locals_))
    right_id = (right // locals_, lax.rem(right, locals_))
    HALO, HALO2, REST, FROM_LOW, FROM_HIGH, PASSED, TOPS, TOPW, SKEL, PART, ROOT, FARS, SHARE = range(KINDS)
    depth = owners // PLANE
    reach = depth // 4
    z, y = o // PLANE, lax.rem(o, PLANE)
    own_row = reach * PLANE
    top_rows = 2 * reach * PLANE
    near_rows = (2 * reach + 1) * PLANE
    below_rows = reach * PLANE
    above_rows = (reach - 1) * PLANE

    def owner_at(dz, dy):
        return lax.rem(z + dz + depth, depth) * PLANE + lax.rem(y + dy, PLANE)

    def beside(n):
        return owner_at(n // PLANE - reach, lax.rem(n, PLANE))


    def load(i, source, target):
        copy = pltpu.make_async_copy(source, target, load_sem.at[i])
        copy.start()
        return copy

    load_owner = load(0, owner_h, owner_v)
    load_member = load(1, member_h, member_v)
    load_vec = load(2, vec, vec_b)
    load_basis = load(3, basis, basis_b)
    load_up = load(4, up, up_b)
    load_root = load(5, root_t, root_b)
    load_top = load(6, top_src_h, top_src)
    load_topb = load(7, top_b, topb_b)
    load_src = load(8, near_src_h, near_src)
    load_near = load(9, near, near_b)
    load_owner_s = load(10, owner_h, owner_s)
    load_count = load(11, count_h, count_s)
    load_far = load(12, far, far_b)

    def remote(source, target, kind, device):
        return pltpu.make_async_remote_copy(
            src_ref=source,
            dst_ref=target,
            send_sem=send_sem.at[REST if kind in (FROM_LOW, FROM_HIGH) else kind],
            recv_sem=recv_sem.at[kind],
            device_id=device,
            device_id_type=MESH,
        )

    def received(ref, kind):
        wait_bytes(ref, recv_sem.at[kind])

    def sent(ref, kind):
        wait_bytes(ref, send_sem.at[kind])

    barrier = pltpu.get_barrier_semaphore()

    def greet(device):
        pl.semaphore_signal(barrier, inc=1, device_id=device, device_id_type=MESH)

    @pl.loop(1, locals_)
    def _(d):
        greet((o, lax.rem(l + d, locals_)))

    greet(left_id)
    greet(right_id)

    @pl.loop(0, own_row)
    def _(n):
        greet((beside(n), l))

    @pl.loop(own_row + 1, near_rows)
    def _(n):
        greet((beside(n), l))

    lane = lax.broadcasted_iota(jnp.int32, (1, WIDE), 1)
    lanes = lax.broadcasted_iota(jnp.int32, (clusters, WIDE), 1)
    key = jnp.where(lanes >= HALF, lanes - HALF, lanes)
    named = jnp.zeros((clusters, WIDE), jnp.int32)
    member = jnp.zeros((clusters, WIDE), jnp.int32)
    load_owner.wait()
    load_member.wait()
    for f in range(slots):
        same = owner_v[:, f : f + 1] == key
        named = jnp.where(same, 1, named)
        member = jnp.where(same, member_v[:, f : f + 1], member)
    second = (lane >= HALF).astype(jnp.int32)
    run = jnp.zeros((1, WIDE), jnp.int32)
    wanted = jnp.zeros((1, WIDE), jnp.int32)
    for t in range(clusters):
        rank_b[t : t + 1, :] = run
        wanted = jnp.where(run == second, wanted + member[t : t + 1], wanted)
        run = run + named[t : t + 1]
    req[own_row] = wanted
    rank_copy = pltpu.make_async_copy(rank_b, rank_s, smem_sem.at[0])
    rank_copy.start()
    tops_row[...] = jnp.zeros((1, WIDE), jnp.int32)
    load_top.wait()
    tops_row[:, 0:2] = top_src[...]
    tops[pl.ds(l, 1), :, :] = tops_row[...].reshape(1, 1, WIDE)

    low = lax.broadcasted_iota(jnp.int32, (NV, WIDE), 1) < HALF
    low_ones = (lax.broadcasted_iota(jnp.int32, (RANK, WIDE), 1) < HALF).astype(jnp.bfloat16)
    high_ones = (lax.broadcasted_iota(jnp.int32, (RANK, WIDE), 1) >= HALF).astype(jnp.bfloat16)
    load_vec.wait()
    load_basis.wait()
    load_up.wait()
    first = l * clusters
    tiles = []
    for t in range(clusters):
        parts = []
        for q in (2 * t, 2 * t + 1):
            block = basis_b[:, q * WIDE : (q + 1) * WIDE]
            diagonal = jnp.concatenate([block * low_ones, block * high_ones], axis=0)
            pair_basis[q] = diagonal
            parts.append(dot_t(vec_b[:, q * WIDE : (q + 1) * WIDE], diagonal))
        leaf_skel = jnp.concatenate(parts, axis=1).astype(jnp.bfloat16)
        block = up_b[:, t * QUAD : (t + 1) * QUAD]
        tile = dot_t(leaf_skel, jnp.concatenate([block, block], axis=0)).astype(jnp.bfloat16)
        skel[pl.ds(first + t, 1), :, :] = tile.reshape(1, NV, WIDE)
        tiles.append(tile.astype(jnp.float32))
    load_root.wait()
    rows = jnp.concatenate(
        [jnp.where(low, tiles[2 * q], tiles[2 * q + 1]) for q in range(clusters // 2)], axis=1
    ).astype(jnp.bfloat16)
    rootward = root_b[...]
    part[pl.ds(l, 1), :, :] = dot_t(rows, jnp.concatenate([rootward, rootward], axis=0)).reshape(1, NV, WIDE)

    load_topb.wait()
    topw[pl.ds(l, 1), :, :] = jnp.concatenate([topb_b[0], topb_b[1]], axis=1).reshape(1, RANK, WIDE)

    pl.semaphore_wait(barrier, near_rows - 1 + locals_ - 1 + 2)

    def share_skeletons():
        @pl.loop(1, locals_)
        def _(d):
            peer = (o, lax.rem(l + d, locals_))
            own = skel.at[pl.ds(first, clusters)]
            remote(own, own, SKEL, peer).start()
            mine = part.at[pl.ds(l, 1)]
            remote(mine, mine, PART, peer).start()

    def ask(begin, end, kind):
        @pl.loop(begin, end)
        def _(n):
            row = (2 * reach - n // PLANE) * PLANE + lax.rem(PLANE - lax.rem(n, PLANE), PLANE)
            remote(req.at[pl.ds(own_row, 1)], req.at[pl.ds(row, 1)], kind, (beside(n), l)).start()

    def pass_up():
        received(req.at[pl.ds(0, PLANE)], FROM_LOW)

        @pl.loop(0, reach)
        def _(k):
            rows = pl.ds(near_rows + k * PLANE, PLANE)
            remote(req.at[pl.ds(0, PLANE)], req.at[rows], PASSED, (owner_at(k + 1, 0), l)).start()

    def pass_down():
        received(req.at[pl.ds(top_rows, PLANE)], FROM_HIGH)

        @pl.loop(0, reach - 1)
        def _(k):
            rows = pl.ds(near_rows + below_rows + k * PLANE, PLANE)
            remote(req.at[pl.ds(top_rows, PLANE)], req.at[rows], PASSED, (owner_at(-k - 1, 0), l)).start()

    away = jnp.minimum(z, depth - z)
    late = away * 4 >= depth + 2 * reach
    middle = (away + 1 >= reach) & (away <= reach + 1)
    rising = z < 2 * reach

    @pl.when(late)
    def _():
        share_skeletons()

    ask(top_rows, near_rows, FROM_LOW)
    ask(0, PLANE, FROM_HIGH)
    for dz in (-reach, reach):
        pl.semaphore_signal(known, inc=1, device_id=(owner_at(dz, 0), l), device_id_type=MESH)

    @pl.when(jnp.logical_not(late))
    def _():
        share_skeletons()

    ask(PLANE, own_row, REST)
    ask(own_row + 1, top_rows, REST)

    edge = REACH * LEAF
    width = leaves * LEAF
    remote(vec_b.at[:, pl.ds(width - edge, edge)], halo.at[0], HALO, right_id).start()
    remote(vec_b.at[:, pl.ds(0, edge)], halo.at[1], HALO2, left_id).start()

    @pl.when(middle & rising)
    def _():
        pass_up()

    @pl.when(middle & jnp.logical_not(rising))
    def _():
        pass_down()

    received(part.at[pl.ds(0, locals_ - 1)], PART)
    root = part[0]
    for other in range(1, locals_):
        root = root + part[other]
    root_tile[...] = root.astype(jnp.bfloat16)
    pl.semaphore_wait(known, 2)

    @pl.when(l == 0)
    def _():
        roots[0] = root_tile[...]

    @pl.when(l != 0)
    def _():
        remote(root_tile, roots.at[0], ROOT, (lax.rem(o + l, owners), l)).start()

    @pl.loop(1, rounds)
    def _(i):
        remote(root_tile, roots.at[i], ROOT, (lax.rem(o + l + locals_ * i, owners), l)).start()

    @pl.when(jnp.logical_not(middle & rising))
    def _():
        pass_up()

    @pl.when(jnp.logical_not(middle & jnp.logical_not(rising)))
    def _():
        pass_down()

    @pl.loop(1, locals_)
    def _(d):
        peer = (o, lax.rem(l + d, locals_))
        mine = tops.at[pl.ds(l, 1)]
        remote(mine, mine, TOPS, peer).start()
        block = topw.at[pl.ds(l, 1)]
        remote(block, block, TOPW, peer).start()

    received(req.at[pl.ds(0, near_rows - 2 * PLANE - 1)], REST)
    received(req.at[pl.ds(0, below_rows + above_rows)], PASSED)
    req_copy = pltpu.make_async_copy(req, req_s, smem_sem.at[1])
    req_copy.start()
    received(skel.at[pl.ds(0, clusters * (locals_ - 1))], SKEL)
    req_copy.wait()

    def chosen(n):
        a = skel[req_s[n, 0, o]].astype(jnp.float32)
        b = skel[req_s[n, 0, HALF + o]].astype(jnp.float32)
        return jnp.where(low, a, b).astype(jnp.bfloat16).reshape(1, NV, WIDE)

    def answer(n, asker):
        far_send[pl.ds(n, 1), :, :] = chosen(n)
        remote(far_send.at[pl.ds(n, 1)], far_recv.at[pl.ds(o, 1)], FARS, (asker, l)).start()

    @pl.loop(0, below_rows)
    def _(i):
        j = below_rows - 1 - i
        answer(near_rows + j, owner_at(-reach - 1 - j // PLANE, lax.rem(j, PLANE)))

    if above_rows:

        @pl.loop(0, above_rows)
        def _(i):
            j = above_rows - 1 - i
            answer(near_rows + below_rows + j, owner_at(reach + 1 + j // PLANE, lax.rem(j, PLANE)))

    @pl.loop(0, own_row)
    def _(n):
        answer(n, beside(n))

    @pl.loop(own_row + 1, near_rows)
    def _(n):
        answer(n, beside(n))

    far_recv[pl.ds(o, 1), :, :] = chosen(own_row)

    received(tops.at[pl.ds(0, locals_ - 1)], TOPS)
    tops_copy = pltpu.make_async_copy(tops, tops_s, smem_sem.at[2])
    tops_copy.start()
    received(topw.at[pl.ds(0, locals_ - 1)], TOPW)
    tops_copy.wait()

    @pl.when(l == 0)
    def _():
        received(roots.at[pl.ds(0, rounds - 1)], ROOT)

    @pl.when(l != 0)
    def _():
        received(roots, ROOT)

    def coupled(s):
        away = lax.rem(o - l - tops_s[s // 2, 0, s % 2] + 2 * owners, owners)
        tile = roots[away // locals_].astype(jnp.float32)
        return jnp.where(lax.rem(away, locals_) == 0, tile, 0.0)

    total_share = jnp.zeros((NV, WIDE), jnp.float32)
    for other in range(locals_):
        lhs = jnp.where(low, coupled(2 * other), coupled(2 * other + 1)).astype(jnp.bfloat16)
        block = topw[other]
        total_share = total_share + dot_t(lhs, jnp.concatenate([block, block], axis=0))
    share[pl.ds(l, 1), :, :] = total_share.reshape(1, NV, WIDE)

    @pl.loop(1, locals_)
    def _(d):
        mine = share.at[pl.ds(l, 1)]
        remote(mine, mine, SHARE, (o, lax.rem(l + d, locals_))).start()

    received(halo.at[0], HALO)
    received(halo.at[1], HALO2)

    def spread(pair, at):
        pair = pair.astype(jnp.float32)
        turned = pltpu.roll(pair, HALF, 1)
        ext[at] = jnp.where(low, pair, turned)
        ext[at + 1] = jnp.where(low, turned, pair)

    for q in range(REACH // 2):
        spread(halo[0, :, q * WIDE : (q + 1) * WIDE], 2 * q)
        spread(halo[1, :, q * WIDE : (q + 1) * WIDE], REACH + leaves + 2 * q)
    for q in range(pairs):
        spread(vec_b[:, q * WIDE : (q + 1) * WIDE], REACH + 2 * q)
    load_src.wait()
    load_near.wait()
    zero = jnp.zeros((NV, WIDE), jnp.float32)

    def quad(pieces):
        rows = [
            jnp.concatenate([jnp.where(low, pieces[0], 0.0), zero], axis=1),
            jnp.concatenate([jnp.where(low, 0.0, pieces[1]), zero], axis=1),
            jnp.concatenate([zero, jnp.where(low, pieces[2], 0.0)], axis=1),
            jnp.concatenate([zero, jnp.where(low, 0.0, pieces[3])], axis=1),
        ]
        return jnp.concatenate(rows, axis=0).astype(jnp.bfloat16)

    offset = REACH - me * leaves

    def inside(at):
        return jnp.minimum(jnp.maximum(at, 0), leaves + 2 * REACH - 1)

    for t in range(clusters):
        acc = jnp.zeros((CLUSTER_LEAVES * NV, LEAF), jnp.float32)
        for i in range(near_slots):
            lhs = quad([ext[inside(near_src[i, CLUSTER_LEAVES * t + c] + offset)] for c in range(CLUSTER_LEAVES)])
            acc = acc + dot_t(lhs, near_b[i, :, t * QUAD : (t + 1) * QUAD])
        for c in range(0, CLUSTER_LEAVES, 2):
            near_res[2 * t + c // 2] = jnp.concatenate(
                [acc[c * NV : (c + 1) * NV], acc[(c + 1) * NV : (c + 2) * NV]], axis=1
            )

    received(share.at[pl.ds(0, locals_ - 1)], SHARE)
    summed = share[0]
    for other in range(1, locals_):
        summed = summed + share[other]
    root_out = summed[:, 0:RANK].astype(jnp.bfloat16)
    downward = dot(root_out, root_b[...])
    rank_copy.wait()
    load_owner_s.wait()
    load_count.wait()
    load_far.wait()

    received(far_recv.at[pl.ds(0, owners - 1)], FARS)

    def picked(t, f):
        source = owner_s[t, f]
        tile = far_recv[source].astype(jnp.float32)
        tile = jnp.where(rank_s[t, source] == t % 2, tile, pltpu.roll(tile, HALF, 1))
        return jnp.where(f < count_s[t], tile, 0.0)

    for g in range(clusters // 4):
        acc = jnp.zeros((4 * NV, RANK), jnp.float32)
        for f in range(slots):
            lhs = quad([picked(4 * g + t, f) for t in range(4)])
            acc = acc + dot_t(lhs, far_b[f, :, g * QUAD : (g + 1) * QUAD])
        for t in range(4):
            at = 4 * g + t
            cluster_out = acc[t * NV : (t + 1) * NV] + downward[:, at * RANK : (at + 1) * RANK]
            leaf_out = dot(cluster_out.astype(jnp.bfloat16), up_b[:, at * QUAD : (at + 1) * QUAD]).astype(jnp.bfloat16)
            for c in range(2):
                q = 2 * at + c
                result = dot(leaf_out[:, c * WIDE : (c + 1) * WIDE], pair_basis[q]) + near_res[q]
                out[:, q * WIDE : (q + 1) * WIDE] = result.astype(jnp.bfloat16)

    sent(skel.at[pl.ds(0, clusters * (locals_ - 1))], SKEL)
    sent(part.at[pl.ds(0, locals_ - 1)], PART)
    sent(req.at[pl.ds(0, near_rows - 1)], REST)
    sent(req.at[pl.ds(0, below_rows + above_rows)], PASSED)
    sent(tops.at[pl.ds(0, locals_ - 1)], TOPS)
    sent(topw.at[pl.ds(0, locals_ - 1)], TOPW)
    sent(halo.at[0], HALO)
    sent(halo.at[1], HALO2)

    @pl.when(l == 0)
    def _():
        sent(roots.at[pl.ds(0, rounds - 1)], ROOT)

    @pl.when(l != 0)
    def _():
        sent(roots, ROOT)

    sent(share.at[pl.ds(0, locals_ - 1)], SHARE)
    sent(far_recv.at[pl.ds(0, owners - 1)], FARS)


def per_device(
    owners,
    locals_,
    vectors,
    leaf_basis,
    near_blocks,
    near_source,
    up_transfer,
    far_owner,
    far_member,
    far_count,
    far_blocks,
    root_transfer,
    top_source,
    top_blocks,
):
    clusters = far_owner.shape[0]
    leaves = clusters * CLUSTER_LEAVES
    bf16, f32, i32 = jnp.bfloat16, jnp.float32, jnp.int32
    hbm = pl.BlockSpec(memory_space=pltpu.HBM)
    vmem = pl.BlockSpec(memory_space=pltpu.VMEM)
    big = (vectors, leaf_basis, near_blocks, up_transfer, far_blocks, root_transfer, top_blocks)
    return pl.pallas_call(
        functools.partial(kernel, owners, locals_),
        out_shape=jax.ShapeDtypeStruct(vectors.shape, bf16),
        in_specs=[hbm] * 12,
        out_specs=vmem,
        scratch_shapes=[pltpu.VMEM(a.shape, bf16) for a in big]
        + [
            pltpu.SMEM((near_source.shape[1], near_source.shape[0]), i32),
            pltpu.SMEM(far_owner.shape, i32),
            pltpu.SMEM(far_count.shape, i32),
            pltpu.VMEM(far_owner.shape, i32),
            pltpu.VMEM(far_owner.shape, i32),
            pltpu.VMEM(top_source.shape, i32),
            pltpu.SemaphoreType.DMA((13,)),
            pltpu.VMEM((leaves // 2, WIDE, WIDE), bf16),
            pltpu.VMEM((leaves + 2 * REACH, NV, WIDE), f32),
            pltpu.VMEM((leaves // 2, NV, WIDE), f32),
            pltpu.VMEM((clusters, WIDE), i32),
            pltpu.SMEM((clusters, WIDE), i32),
            pltpu.VMEM((2, NV, REACH * LEAF), bf16),
            pltpu.VMEM((owners, 1, WIDE), i32),
            pltpu.SMEM((owners, 1, WIDE), i32),
            pltpu.VMEM((1, WIDE), i32),
            pltpu.VMEM((locals_, 1, WIDE), i32),
            pltpu.SMEM((locals_, 1, WIDE), i32),
            pltpu.VMEM((locals_, RANK, WIDE), bf16),
            pltpu.VMEM((clusters * locals_, NV, WIDE), bf16),
            pltpu.VMEM((locals_, NV, WIDE), f32),
            pltpu.VMEM((NV, WIDE), bf16),
            pltpu.VMEM((owners // locals_, NV, WIDE), bf16),
            pltpu.VMEM((owners, NV, WIDE), bf16),
            pltpu.VMEM((owners, NV, WIDE), bf16),
            pltpu.VMEM((locals_, NV, WIDE), f32),
            pltpu.SemaphoreType.DMA((3,)),
            pltpu.SemaphoreType.DMA((KINDS,)),
            pltpu.SemaphoreType.DMA((KINDS,)),
            pltpu.SemaphoreType.REGULAR,
        ],
        compiler_params=pltpu.CompilerParams(
            collective_id=0, has_side_effects=True, vmem_limit_bytes=63 * 1024 * 1024
        ),
    )(*big, near_source.T, far_owner, far_member, far_count, top_source)


def solution(mesh):
    return jax.shard_map(
        functools.partial(per_device, mesh.shape["owner"], mesh.shape["local"]),
        mesh=mesh,
        in_specs=(
            P(None, ("owner", "local")),
            P(None, ("owner", "local")),
            P(None, None, ("owner", "local")),
            P(("owner", "local"), None),
            P(None, ("owner", "local")),
            P(("owner", "local"), None),
            P(("owner", "local"), None),
            P(("owner", "local")),
            P(None, None, ("owner", "local")),
            P(None, ("owner", "local")),
            P("owner", "local"),
            P("local", None, "owner"),
        ),
        out_specs=P(None, ("owner", "local")),
        check_vma=False,
    )
```

```python
import functools

import jax
import jax.numpy as jnp
from jax import lax
from jax.experimental import pallas as pl
from jax.experimental.pallas import tpu as pltpu
from jax.sharding import PartitionSpec as P

MESH = pl.DeviceIdType.MESH
KINDS = 13
NV = 8
LEAF = 64
RANK = 64
CLUSTER_LEAVES = 4
REACH = 4
HALF = 64
PLANE = 4
WIDE = 128
QUAD = 256


def dot(left, right):
    return jnp.dot(left, right, preferred_element_type=jnp.float32)


def dot_t(left, right):
    return lax.dot_general(left, right, (((1,), (1,)), ((), ())), preferred_element_type=jnp.float32)


def wait_bytes(ref, sem):
    pltpu.make_async_copy(ref, ref, sem).wait()


def kernel(
    owners,
    locals_,
    vec,
    basis,
    near,
    up,
    far,
    root_t,
    top_b,
    near_src_h,
    owner_h,
    member_h,
    count_h,
    top_src_h,
    out,
    vec_b,
    basis_b,
    near_b,
    up_b,
    far_b,
    root_b,
    topb_b,
    near_src,
    owner_s,
    count_s,
    owner_v,
    member_v,
    top_src,
    load_sem,
    pair_basis,
    ext,
    near_res,
    rank_b,
    rank_s,
    halo,
    req,
    req_s,
    tops_row,
    tops,
    tops_s,
    topw,
    skel,
    part,
    root_tile,
    roots,
    far_send,
    far_recv,
    share,
    smem_sem,
    send_sem,
    recv_sem,
    known,
):
    o, l = lax.axis_index("owner"), lax.axis_index("local")
    me = o * locals_ + l
    total = owners * locals_
    clusters = skel.shape[0] // locals_
    slots = far_b.shape[0]
    near_slots = near_b.shape[0]
    leaves = clusters * CLUSTER_LEAVES
    pairs = leaves // 2
    rounds = owners // locals_
    left, right = lax.rem(me + total - 1, total), lax.rem(me + 1, total)
    left_id = (left // locals_, lax.rem(left, locals_))
    right_id = (right // locals_, lax.rem(right, locals_))
    HALO, HALO2, REST, FROM_LOW, FROM_HIGH, PASSED, TOPS, TOPW, SKEL, PART, ROOT, FARS, SHARE = range(KINDS)
    depth = owners // PLANE
    reach = depth // 4
    z, y = o // PLANE, lax.rem(o, PLANE)
    own_row = reach * PLANE
    top_rows = 2 * reach * PLANE
    near_rows = (2 * reach + 1) * PLANE
    below_rows = reach * PLANE
    above_rows = (reach - 1) * PLANE

    def owner_at(dz, dy):
        return lax.rem(z + dz + depth, depth) * PLANE + lax.rem(y + dy, PLANE)

    def beside(n):
        return owner_at(n // PLANE - reach, lax.rem(n, PLANE))


    def remote(source, target, kind, device):
        return pltpu.make_async_remote_copy(
            src_ref=source,
            dst_ref=target,
            send_sem=send_sem.at[REST if kind in (FROM_LOW, FROM_HIGH) else kind],
            recv_sem=recv_sem.at[kind],
            device_id=device,
            device_id_type=MESH,
        )

    def received(ref, kind):
        wait_bytes(ref, recv_sem.at[kind])

    def sent(ref, kind):
        wait_bytes(ref, send_sem.at[kind])

    barrier = pltpu.get_barrier_semaphore()

    def greet(device):
        pl.semaphore_signal(barrier, inc=1, device_id=device, device_id_type=MESH)

    def greet_planes(begin, end):
        @pl.loop(begin, end, unroll=True)
        def _(n):
            greet((beside(n), l))

    greet_planes(0, PLANE)
    greet_planes(top_rows, near_rows)
    greet_planes(PLANE, own_row)
    greet_planes(own_row + 1, top_rows)

    @pl.loop(1, locals_, unroll=True)
    def _(d):
        greet((o, lax.rem(l + d, locals_)))

    greet(left_id)
    greet(right_id)

    def load(i, source, target):
        copy = pltpu.make_async_copy(source, target, load_sem.at[i])
        copy.start()
        return copy

    load_owner = load(0, owner_h, owner_v)
    load_member = load(1, member_h, member_v)
    load_vec = load(2, vec, vec_b)
    load_basis = load(3, basis, basis_b)
    load_up = load(4, up, up_b)
    load_root = load(5, root_t, root_b)
    load_top = load(6, top_src_h, top_src)
    load_topb = load(7, top_b, topb_b)
    load_src = load(8, near_src_h, near_src)
    load_near = load(9, near, near_b)
    load_owner_s = load(10, owner_h, owner_s)
    load_count = load(11, count_h, count_s)
    load_far = load(12, far, far_b)

    lane = lax.broadcasted_iota(jnp.int32, (1, WIDE), 1)
    lanes = lax.broadcasted_iota(jnp.int32, (clusters, WIDE), 1)
    key = jnp.where(lanes >= HALF, lanes - HALF, lanes)
    named = jnp.zeros((clusters, WIDE), jnp.int32)
    member = jnp.zeros((clusters, WIDE), jnp.int32)
    load_owner.wait()
    load_member.wait()
    for f in range(slots):
        same = owner_v[:, f : f + 1] == key
        named = jnp.where(same, 1, named)
        member = jnp.where(same, member_v[:, f : f + 1], member)
    second = (lane >= HALF).astype(jnp.int32)
    run = jnp.zeros((1, WIDE), jnp.int32)
    wanted = jnp.zeros((1, WIDE), jnp.int32)
    for t in range(clusters):
        rank_b[t : t + 1, :] = run
        wanted = jnp.where(run == second, wanted + member[t : t + 1], wanted)
        run = run + named[t : t + 1]
    req[own_row] = wanted
    rank_copy = pltpu.make_async_copy(rank_b, rank_s, smem_sem.at[0])
    rank_copy.start()
    tops_row[...] = jnp.zeros((1, WIDE), jnp.int32)
    load_top.wait()
    tops_row[:, 0:2] = top_src[...]
    tops[pl.ds(l, 1), :, :] = tops_row[...].reshape(1, 1, WIDE)

    low = lax.broadcasted_iota(jnp.int32, (NV, WIDE), 1) < HALF
    low_ones = (lax.broadcasted_iota(jnp.int32, (RANK, WIDE), 1) < HALF).astype(jnp.bfloat16)
    high_ones = (lax.broadcasted_iota(jnp.int32, (RANK, WIDE), 1) >= HALF).astype(jnp.bfloat16)
    load_vec.wait()
    load_basis.wait()
    load_up.wait()
    first = l * clusters
    tiles = []
    for t in range(clusters):
        parts = []
        for q in (2 * t, 2 * t + 1):
            block = basis_b[:, q * WIDE : (q + 1) * WIDE]
            diagonal = jnp.concatenate([block * low_ones, block * high_ones], axis=0)
            pair_basis[q] = diagonal
            parts.append(dot_t(vec_b[:, q * WIDE : (q + 1) * WIDE], diagonal))
        leaf_skel = jnp.concatenate(parts, axis=1).astype(jnp.bfloat16)
        block = up_b[:, t * QUAD : (t + 1) * QUAD]
        tile = dot_t(leaf_skel, jnp.concatenate([block, block], axis=0)).astype(jnp.bfloat16)
        skel[pl.ds(first + t, 1), :, :] = tile.reshape(1, NV, WIDE)
        tiles.append(tile.astype(jnp.float32))
    load_root.wait()
    rows = jnp.concatenate(
        [jnp.where(low, tiles[2 * q], tiles[2 * q + 1]) for q in range(clusters // 2)], axis=1
    ).astype(jnp.bfloat16)
    rootward = root_b[...]
    part[pl.ds(l, 1), :, :] = dot_t(rows, jnp.concatenate([rootward, rootward], axis=0)).reshape(1, NV, WIDE)

    load_topb.wait()
    topw[pl.ds(l, 1), :, :] = jnp.concatenate([topb_b[0], topb_b[1]], axis=1).reshape(1, RANK, WIDE)

    pl.semaphore_wait(barrier, near_rows - 1 + locals_ - 1 + 2)

    def share_skeletons():
        @pl.loop(1, locals_, unroll=True)
        def _(d):
            mine = part.at[pl.ds(l, 1)]
            remote(mine, mine, PART, (o, lax.rem(l + d, locals_))).start()

        @pl.loop(1, locals_, unroll=True)
        def _(d):
            own = skel.at[pl.ds(first, clusters)]
            remote(own, own, SKEL, (o, lax.rem(l + d, locals_))).start()

    def ask(begin, end, kind):
        @pl.loop(begin, end, unroll=True)
        def _(n):
            row = (2 * reach - n // PLANE) * PLANE + lax.rem(PLANE - lax.rem(n, PLANE), PLANE)
            remote(req.at[own_row], req.at[row], kind, (beside(n), l)).start()

    def pass_up():
        received(req.at[pl.ds(0, PLANE)], FROM_LOW)

        @pl.loop(0, reach, unroll=True)
        def _(k):
            rows = pl.ds(near_rows + k * PLANE, PLANE)
            remote(req.at[pl.ds(0, PLANE)], req.at[rows], PASSED, (owner_at(k + 1, 0), l)).start()

    def pass_down():
        received(req.at[pl.ds(top_rows, PLANE)], FROM_HIGH)

        @pl.loop(0, reach - 1, unroll=True)
        def _(k):
            rows = pl.ds(near_rows + below_rows + k * PLANE, PLANE)
            remote(req.at[pl.ds(top_rows, PLANE)], req.at[rows], PASSED, (owner_at(-k - 1, 0), l)).start()

    away = jnp.minimum(z, depth - z)
    late = away * 4 >= depth + 2 * reach
    middle = (away + 1 >= reach) & (away <= reach + 1)
    rising = z < 2 * reach

    @pl.when(late)
    def _():
        share_skeletons()

    ask(top_rows, near_rows, FROM_LOW)
    ask(0, PLANE, FROM_HIGH)
    for dz in (-reach, reach):
        pl.semaphore_signal(known, inc=1, device_id=(owner_at(dz, 0), l), device_id_type=MESH)

    @pl.when(jnp.logical_not(late))
    def _():
        share_skeletons()

    ask(PLANE, own_row, REST)
    ask(own_row + 1, top_rows, REST)

    edge = REACH * LEAF
    width = leaves * LEAF
    remote(vec_b.at[:, pl.ds(width - edge, edge)], halo.at[0], HALO, right_id).start()
    remote(vec_b.at[:, pl.ds(0, edge)], halo.at[1], HALO2, left_id).start()

    @pl.when(middle & rising)
    def _():
        pass_up()

    @pl.when(middle & jnp.logical_not(rising))
    def _():
        pass_down()

    received(part.at[pl.ds(0, locals_ - 1)], PART)
    root = part[0]
    for other in range(1, locals_):
        root = root + part[other]
    root_tile[...] = root.astype(jnp.bfloat16)
    pl.semaphore_wait(known, 2)

    @pl.when(l == 0)
    def _():
        roots[0] = root_tile[...]

    @pl.when(l != 0)
    def _():
        remote(root_tile, roots.at[0], ROOT, (lax.rem(o + l, owners), l)).start()

    @pl.loop(1, rounds, unroll=True)
    def _(i):
        remote(root_tile, roots.at[i], ROOT, (lax.rem(o + l + locals_ * i, owners), l)).start()

    @pl.when(jnp.logical_not(middle & rising))
    def _():
        pass_up()

    @pl.when(jnp.logical_not(middle & jnp.logical_not(rising)))
    def _():
        pass_down()

    @pl.loop(1, locals_, unroll=True)
    def _(d):
        peer = (o, lax.rem(l + d, locals_))
        mine = tops.at[pl.ds(l, 1)]
        remote(mine, mine, TOPS, peer).start()
        block = topw.at[pl.ds(l, 1)]
        remote(block, block, TOPW, peer).start()

    def to_scalars(rows, sem):
        copy = pltpu.make_async_copy(req.at[rows], req_s.at[rows], sem)
        copy.start()
        return copy

    received(req.at[pl.ds(0, near_rows - 2 * PLANE - 1)], REST)
    near_asked = to_scalars(pl.ds(0, near_rows), smem_sem.at[1])
    received(skel.at[pl.ds(0, clusters * (locals_ - 1))], SKEL)
    near_asked.wait()

    def chosen(n):
        a = skel[req_s[n, 0, o]].astype(jnp.float32)
        b = skel[req_s[n, 0, HALF + o]].astype(jnp.float32)
        return jnp.where(low, a, b).astype(jnp.bfloat16).reshape(1, NV, WIDE)

    def answer(n, asker):
        far_send[pl.ds(n, 1), :, :] = chosen(n)
        remote(far_send.at[pl.ds(n, 1)], far_recv.at[pl.ds(o, 1)], FARS, (asker, l)).start()

    @pl.loop(0, own_row, unroll=True)
    def _(n):
        answer(n, beside(n))

    @pl.loop(own_row + 1, near_rows, unroll=True)
    def _(n):
        answer(n, beside(n))

    received(req.at[pl.ds(0, below_rows + above_rows)], PASSED)
    far_asked = to_scalars(pl.ds(near_rows, below_rows + above_rows), smem_sem.at[3])
    far_asked.wait()

    @pl.loop(0, below_rows, unroll=True)
    def _(i):
        j = below_rows - 1 - i
        answer(near_rows + j, owner_at(-reach - 1 - j // PLANE, lax.rem(j, PLANE)))

    if above_rows:

        @pl.loop(0, above_rows, unroll=True)
        def _(i):
            j = above_rows - 1 - i
            answer(near_rows + below_rows + j, owner_at(reach + 1 + j // PLANE, lax.rem(j, PLANE)))

    far_recv[pl.ds(o, 1), :, :] = chosen(own_row)

    received(tops.at[pl.ds(0, locals_ - 1)], TOPS)
    tops_copy = pltpu.make_async_copy(tops, tops_s, smem_sem.at[2])
    tops_copy.start()
    received(topw.at[pl.ds(0, locals_ - 1)], TOPW)
    tops_copy.wait()

    @pl.when(l == 0)
    def _():
        received(roots.at[pl.ds(0, rounds - 1)], ROOT)

    @pl.when(l != 0)
    def _():
        received(roots, ROOT)

    def coupled(s):
        away = lax.rem(o - l - tops_s[s // 2, 0, s % 2] + 2 * owners, owners)
        tile = roots[away // locals_].astype(jnp.float32)
        return jnp.where(lax.rem(away, locals_) == 0, tile, 0.0)

    total_share = jnp.zeros((NV, WIDE), jnp.float32)
    for other in range(locals_):
        lhs = jnp.where(low, coupled(2 * other), coupled(2 * other + 1)).astype(jnp.bfloat16)
        block = topw[other]
        total_share = total_share + dot_t(lhs, jnp.concatenate([block, block], axis=0))
    share[pl.ds(l, 1), :, :] = total_share.reshape(1, NV, WIDE)

    @pl.loop(1, locals_, unroll=True)
    def _(d):
        mine = share.at[pl.ds(l, 1)]
        remote(mine, mine, SHARE, (o, lax.rem(l + d, locals_))).start()

    received(halo.at[0], HALO)
    received(halo.at[1], HALO2)

    def spread(pair, at):
        pair = pair.astype(jnp.float32)
        turned = pltpu.roll(pair, HALF, 1)
        ext[at] = jnp.where(low, pair, turned)
        ext[at + 1] = jnp.where(low, turned, pair)

    for q in range(REACH // 2):
        spread(halo[0, :, q * WIDE : (q + 1) * WIDE], 2 * q)
        spread(halo[1, :, q * WIDE : (q + 1) * WIDE], REACH + leaves + 2 * q)
    for q in range(pairs):
        spread(vec_b[:, q * WIDE : (q + 1) * WIDE], REACH + 2 * q)
    load_src.wait()
    load_near.wait()
    zero = jnp.zeros((NV, WIDE), jnp.float32)

    def quad(pieces):
        rows = [
            jnp.concatenate([jnp.where(low, pieces[0], 0.0), zero], axis=1),
            jnp.concatenate([jnp.where(low, 0.0, pieces[1]), zero], axis=1),
            jnp.concatenate([zero, jnp.where(low, pieces[2], 0.0)], axis=1),
            jnp.concatenate([zero, jnp.where(low, 0.0, pieces[3])], axis=1),
        ]
        return jnp.concatenate(rows, axis=0).astype(jnp.bfloat16)

    offset = REACH - me * leaves

    def inside(at):
        return jnp.minimum(jnp.maximum(at, 0), leaves + 2 * REACH - 1)

    for t in range(clusters):
        acc = jnp.zeros((CLUSTER_LEAVES * NV, LEAF), jnp.float32)
        for i in range(near_slots):
            lhs = quad([ext[inside(near_src[i, CLUSTER_LEAVES * t + c] + offset)] for c in range(CLUSTER_LEAVES)])
            acc = acc + dot_t(lhs, near_b[i, :, t * QUAD : (t + 1) * QUAD])
        for c in range(0, CLUSTER_LEAVES, 2):
            near_res[2 * t + c // 2] = jnp.concatenate(
                [acc[c * NV : (c + 1) * NV], acc[(c + 1) * NV : (c + 2) * NV]], axis=1
            )

    received(share.at[pl.ds(0, locals_ - 1)], SHARE)
    summed = share[0]
    for other in range(1, locals_):
        summed = summed + share[other]
    root_out = summed[:, 0:RANK].astype(jnp.bfloat16)
    downward = dot(root_out, root_b[...])
    rank_copy.wait()
    load_owner_s.wait()
    load_count.wait()
    load_far.wait()

    received(far_recv.at[pl.ds(0, owners - 1)], FARS)

    def picked(t, f):
        source = owner_s[t, f]
        tile = far_recv[source].astype(jnp.float32)
        tile = jnp.where(rank_s[t, source] == t % 2, tile, pltpu.roll(tile, HALF, 1))
        return jnp.where(f < count_s[t], tile, 0.0)

    for g in range(clusters // 4):
        acc = jnp.zeros((4 * NV, RANK), jnp.float32)
        for f in range(slots):
            lhs = quad([picked(4 * g + t, f) for t in range(4)])
            acc = acc + dot_t(lhs, far_b[f, :, g * QUAD : (g + 1) * QUAD])
        for t in range(4):
            at = 4 * g + t
            cluster_out = acc[t * NV : (t + 1) * NV] + downward[:, at * RANK : (at + 1) * RANK]
            leaf_out = dot(cluster_out.astype(jnp.bfloat16), up_b[:, at * QUAD : (at + 1) * QUAD]).astype(jnp.bfloat16)
            for c in range(2):
                q = 2 * at + c
                result = dot(leaf_out[:, c * WIDE : (c + 1) * WIDE], pair_basis[q]) + near_res[q]
                out[:, q * WIDE : (q + 1) * WIDE] = result.astype(jnp.bfloat16)

    sent(skel.at[pl.ds(0, clusters * (locals_ - 1))], SKEL)
    sent(part.at[pl.ds(0, locals_ - 1)], PART)
    sent(req.at[pl.ds(0, near_rows - 1)], REST)
    sent(req.at[pl.ds(0, below_rows + above_rows)], PASSED)
    sent(tops.at[pl.ds(0, locals_ - 1)], TOPS)
    sent(topw.at[pl.ds(0, locals_ - 1)], TOPW)
    sent(halo.at[0], HALO)
    sent(halo.at[1], HALO2)

    @pl.when(l == 0)
    def _():
        sent(roots.at[pl.ds(0, rounds - 1)], ROOT)

    @pl.when(l != 0)
    def _():
        sent(roots, ROOT)

    sent(share.at[pl.ds(0, locals_ - 1)], SHARE)
    sent(far_recv.at[pl.ds(0, owners - 1)], FARS)


def per_device(
    owners,
    locals_,
    vectors,
    leaf_basis,
    near_blocks,
    near_source,
    up_transfer,
    far_owner,
    far_member,
    far_count,
    far_blocks,
    root_transfer,
    top_source,
    top_blocks,
):
    clusters = far_owner.shape[0]
    leaves = clusters * CLUSTER_LEAVES
    bf16, f32, i32 = jnp.bfloat16, jnp.float32, jnp.int32
    hbm = pl.BlockSpec(memory_space=pltpu.HBM)
    vmem = pl.BlockSpec(memory_space=pltpu.VMEM)
    big = (vectors, leaf_basis, near_blocks, up_transfer, far_blocks, root_transfer, top_blocks)
    return pl.pallas_call(
        functools.partial(kernel, owners, locals_),
        out_shape=jax.ShapeDtypeStruct(vectors.shape, bf16),
        in_specs=[hbm] * 12,
        out_specs=vmem,
        scratch_shapes=[pltpu.VMEM(a.shape, bf16) for a in big]
        + [
            pltpu.SMEM((near_source.shape[1], near_source.shape[0]), i32),
            pltpu.SMEM(far_owner.shape, i32),
            pltpu.SMEM(far_count.shape, i32),
            pltpu.VMEM(far_owner.shape, i32),
            pltpu.VMEM(far_owner.shape, i32),
            pltpu.VMEM(top_source.shape, i32),
            pltpu.SemaphoreType.DMA((13,)),
            pltpu.VMEM((leaves // 2, WIDE, WIDE), bf16),
            pltpu.VMEM((leaves + 2 * REACH, NV, WIDE), f32),
            pltpu.VMEM((leaves // 2, NV, WIDE), f32),
            pltpu.VMEM((clusters, WIDE), i32),
            pltpu.SMEM((clusters, WIDE), i32),
            pltpu.VMEM((2, NV, REACH * LEAF), bf16),
            pltpu.VMEM((owners, 1, WIDE), i32),
            pltpu.SMEM((owners, 1, WIDE), i32),
            pltpu.VMEM((1, WIDE), i32),
            pltpu.VMEM((locals_, 1, WIDE), i32),
            pltpu.SMEM((locals_, 1, WIDE), i32),
            pltpu.VMEM((locals_, RANK, WIDE), bf16),
            pltpu.VMEM((clusters * locals_, NV, WIDE), bf16),
            pltpu.VMEM((locals_, NV, WIDE), f32),
            pltpu.VMEM((NV, WIDE), bf16),
            pltpu.VMEM((owners // locals_, NV, WIDE), bf16),
            pltpu.VMEM((owners, NV, WIDE), bf16),
            pltpu.VMEM((owners, NV, WIDE), bf16),
            pltpu.VMEM((locals_, NV, WIDE), f32),
            pltpu.SemaphoreType.DMA((4,)),
            pltpu.SemaphoreType.DMA((KINDS,)),
            pltpu.SemaphoreType.DMA((KINDS,)),
            pltpu.SemaphoreType.REGULAR,
        ],
        compiler_params=pltpu.CompilerParams(
            collective_id=0, has_side_effects=True, vmem_limit_bytes=63 * 1024 * 1024
        ),
    )(*big, near_source.T, far_owner, far_member, far_count, top_source)


def solution(mesh):
    return jax.shard_map(
        functools.partial(per_device, mesh.shape["owner"], mesh.shape["local"]),
        mesh=mesh,
        in_specs=(
            P(None, ("owner", "local")),
            P(None, ("owner", "local")),
            P(None, None, ("owner", "local")),
            P(("owner", "local"), None),
            P(None, ("owner", "local")),
            P(("owner", "local"), None),
            P(("owner", "local"), None),
            P(("owner", "local")),
            P(None, None, ("owner", "local")),
            P(None, ("owner", "local")),
            P("owner", "local"),
            P("local", None, "owner"),
        ),
        out_specs=P(None, ("owner", "local")),
        check_vma=False,
    )
```

```python
import functools

import jax
import jax.numpy as jnp
from jax import lax
from jax.experimental import pallas as pl
from jax.experimental.pallas import tpu as pltpu
from jax.sharding import PartitionSpec as P

MESH = pl.DeviceIdType.MESH
KINDS = 13
NV = 8
LEAF = 64
RANK = 64
CLUSTER_LEAVES = 4
REACH = 4
HALF = 64
PLANE = 4
WIDE = 128
QUAD = 256


def dot(left, right):
    return jnp.dot(left, right, preferred_element_type=jnp.float32)


def dot_t(left, right):
    return lax.dot_general(left, right, (((1,), (1,)), ((), ())), preferred_element_type=jnp.float32)


def wait_bytes(ref, sem):
    pltpu.make_async_copy(ref, ref, sem).wait()


def kernel(
    owners,
    locals_,
    vec,
    basis,
    near,
    up,
    far,
    root_t,
    top_b,
    near_src_h,
    owner_h,
    member_h,
    count_h,
    top_src_h,
    out,
    vec_b,
    basis_b,
    near_b,
    up_b,
    far_b,
    root_b,
    topb_b,
    near_src,
    owner_s,
    count_s,
    owner_v,
    member_v,
    top_src,
    load_sem,
    pair_basis,
    ext,
    near_res,
    rank_b,
    rank_s,
    halo,
    req,
    req_s,
    tops_row,
    tops,
    tops_s,
    topw,
    skel,
    skel_rows,
    part,
    root_tile,
    roots,
    far_send,
    far_recv,
    share,
    smem_sem,
    send_sem,
    recv_sem,
    known,
):
    o, l = lax.axis_index("owner"), lax.axis_index("local")
    me = o * locals_ + l
    total = owners * locals_
    clusters = skel.shape[0] // locals_
    slots = far_b.shape[0]
    near_slots = near_b.shape[0]
    leaves = clusters * CLUSTER_LEAVES
    pairs = leaves // 2
    rounds = owners // locals_
    left, right = lax.rem(me + total - 1, total), lax.rem(me + 1, total)
    left_id = (left // locals_, lax.rem(left, locals_))
    right_id = (right // locals_, lax.rem(right, locals_))
    HALO, HALO2, REST, FROM_LOW, FROM_HIGH, PASSED, TOPS, TOPW, SKEL, PART, ROOT, FARS, SHARE = range(KINDS)
    depth = owners // PLANE
    reach = depth // 4
    z, y = o // PLANE, lax.rem(o, PLANE)
    own_row = reach * PLANE
    top_rows = 2 * reach * PLANE
    near_rows = (2 * reach + 1) * PLANE
    below_rows = reach * PLANE
    above_rows = (reach - 1) * PLANE

    def owner_at(dz, dy):
        return lax.rem(z + dz + depth, depth) * PLANE + lax.rem(y + dy, PLANE)

    def beside(n):
        return owner_at(n // PLANE - reach, lax.rem(n, PLANE))


    def remote(source, target, kind, device):
        return pltpu.make_async_remote_copy(
            src_ref=source,
            dst_ref=target,
            send_sem=send_sem.at[REST if kind in (FROM_LOW, FROM_HIGH) else kind],
            recv_sem=recv_sem.at[kind],
            device_id=device,
            device_id_type=MESH,
        )

    def received(ref, kind):
        wait_bytes(ref, recv_sem.at[kind])

    def sent(ref, kind):
        wait_bytes(ref, send_sem.at[kind])

    barrier = pltpu.get_barrier_semaphore()

    def greet(device):
        pl.semaphore_signal(barrier, inc=1, device_id=device, device_id_type=MESH)

    def greet_planes(begin, end):
        @pl.loop(begin, end, unroll=True)
        def _(n):
            greet((beside(n), l))

    greet_planes(0, PLANE)
    greet_planes(top_rows, near_rows)
    greet_planes(PLANE, own_row)
    greet_planes(own_row + 1, top_rows)

    @pl.loop(1, locals_, unroll=True)
    def _(d):
        greet((o, lax.rem(l + d, locals_)))

    greet(left_id)
    greet(right_id)

    def load(i, source, target):
        copy = pltpu.make_async_copy(source, target, load_sem.at[i])
        copy.start()
        return copy

    load_owner = load(0, owner_h, owner_v)
    load_member = load(1, member_h, member_v)
    load_vec = load(2, vec, vec_b)
    load_basis = load(3, basis, basis_b)
    load_up = load(4, up, up_b)
    load_root = load(5, root_t, root_b)
    load_top = load(6, top_src_h, top_src)
    load_topb = load(7, top_b, topb_b)
    load_src = load(8, near_src_h, near_src)
    load_near = load(9, near, near_b)
    load_owner_s = load(10, owner_h, owner_s)
    load_count = load(11, count_h, count_s)
    load_far = load(12, far, far_b)

    lane = lax.broadcasted_iota(jnp.int32, (1, WIDE), 1)
    lanes = lax.broadcasted_iota(jnp.int32, (clusters, WIDE), 1)
    key = jnp.where(lanes >= HALF, lanes - HALF, lanes)
    named = jnp.zeros((clusters, WIDE), jnp.int32)
    member = jnp.zeros((clusters, WIDE), jnp.int32)
    load_owner.wait()
    load_member.wait()
    for f in range(slots):
        same = owner_v[:, f : f + 1] == key
        named = jnp.where(same, 1, named)
        member = jnp.where(same, member_v[:, f : f + 1], member)
    second = (lane >= HALF).astype(jnp.int32)
    run = jnp.zeros((1, WIDE), jnp.int32)
    wanted = jnp.zeros((1, WIDE), jnp.int32)
    for t in range(clusters):
        rank_b[t : t + 1, :] = run
        wanted = jnp.where(run == second, wanted + member[t : t + 1], wanted)
        run = run + named[t : t + 1]
    req[own_row] = wanted
    rank_copy = pltpu.make_async_copy(rank_b, rank_s, smem_sem.at[0])
    rank_copy.start()
    tops_row[...] = jnp.zeros((1, WIDE), jnp.int32)
    load_top.wait()
    tops_row[:, 0:2] = top_src[...]
    tops[pl.ds(l, 1), :, :] = tops_row[...].reshape(1, 1, WIDE)

    low = lax.broadcasted_iota(jnp.int32, (NV, WIDE), 1) < HALF
    low_ones = (lax.broadcasted_iota(jnp.int32, (RANK, WIDE), 1) < HALF).astype(jnp.bfloat16)
    high_ones = (lax.broadcasted_iota(jnp.int32, (RANK, WIDE), 1) >= HALF).astype(jnp.bfloat16)
    load_vec.wait()
    load_basis.wait()
    load_up.wait()
    first = l * clusters

    @pl.loop(0, clusters)
    def _(t):
        parts = []
        for c in range(2):
            q = 2 * t + c
            lanes_q = pl.ds(pl.multiple_of(q * WIDE, WIDE), WIDE)
            block = basis_b[:, lanes_q]
            diagonal = jnp.concatenate([block * low_ones, block * high_ones], axis=0)
            pair_basis[q] = diagonal
            parts.append(dot_t(vec_b[:, lanes_q], diagonal))
        leaf_skel = jnp.concatenate(parts, axis=1).astype(jnp.bfloat16)
        block = up_b[:, pl.ds(pl.multiple_of(t * QUAD, QUAD), QUAD)]
        tile = dot_t(leaf_skel, jnp.concatenate([block, block], axis=0)).astype(jnp.bfloat16)
        skel[pl.ds(first + t, 1), :, :] = tile.reshape(1, NV, WIDE)

    tiles = [skel[first + t].astype(jnp.float32) for t in range(clusters)]
    load_root.wait()
    rows = jnp.concatenate(
        [jnp.where(low, tiles[2 * q], tiles[2 * q + 1]) for q in range(clusters // 2)], axis=1
    ).astype(jnp.bfloat16)
    rootward = root_b[...]
    part[pl.ds(l, 1), :, :] = dot_t(rows, jnp.concatenate([rootward, rootward], axis=0)).reshape(1, NV, WIDE)

    load_topb.wait()
    topw[pl.ds(l, 1), :, :] = jnp.concatenate([topb_b[0], topb_b[1]], axis=1).reshape(1, RANK, WIDE)

    pl.semaphore_wait(barrier, near_rows - 1 + locals_ - 1 + 2)

    def share_skeletons():
        @pl.loop(1, locals_, unroll=True)
        def _(d):
            mine = part.at[pl.ds(l, 1)]
            remote(mine, mine, PART, (o, lax.rem(l + d, locals_))).start()

        @pl.loop(1, locals_, unroll=True)
        def _(d):
            own = skel.at[pl.ds(first, clusters)]
            remote(own, own, SKEL, (o, lax.rem(l + d, locals_))).start()

    def ask(begin, end, kind):
        @pl.loop(begin, end, unroll=True)
        def _(n):
            row = (2 * reach - n // PLANE) * PLANE + lax.rem(PLANE - lax.rem(n, PLANE), PLANE)
            remote(req.at[own_row], req.at[row], kind, (beside(n), l)).start()

    def pass_up():
        received(req.at[pl.ds(0, PLANE)], FROM_LOW)

        @pl.loop(0, reach, unroll=True)
        def _(k):
            rows = pl.ds(near_rows + k * PLANE, PLANE)
            remote(req.at[pl.ds(0, PLANE)], req.at[rows], PASSED, (owner_at(k + 1, 0), l)).start()

    def pass_down():
        received(req.at[pl.ds(top_rows, PLANE)], FROM_HIGH)

        @pl.loop(0, reach - 1, unroll=True)
        def _(k):
            rows = pl.ds(near_rows + below_rows + k * PLANE, PLANE)
            remote(req.at[pl.ds(top_rows, PLANE)], req.at[rows], PASSED, (owner_at(-k - 1, 0), l)).start()

    away = jnp.minimum(z, depth - z)
    late = away * 4 >= depth + 2 * reach
    middle = (away + 1 >= reach) & (away <= reach + 1)
    rising = z < 2 * reach

    @pl.when(late)
    def _():
        share_skeletons()

    ask(top_rows, near_rows, FROM_LOW)
    ask(0, PLANE, FROM_HIGH)
    for dz in (-reach, reach):
        pl.semaphore_signal(known, inc=1, device_id=(owner_at(dz, 0), l), device_id_type=MESH)

    @pl.when(jnp.logical_not(late))
    def _():
        share_skeletons()

    ask(PLANE, own_row, REST)
    ask(own_row + 1, top_rows, REST)

    edge = REACH * LEAF
    width = leaves * LEAF
    remote(vec_b.at[:, pl.ds(width - edge, edge)], halo.at[0], HALO, right_id).start()
    remote(vec_b.at[:, pl.ds(0, edge)], halo.at[1], HALO2, left_id).start()

    @pl.when(middle & rising)
    def _():
        pass_up()

    @pl.when(middle & jnp.logical_not(rising))
    def _():
        pass_down()

    received(part.at[pl.ds(0, locals_ - 1)], PART)
    root = part[0]
    for other in range(1, locals_):
        root = root + part[other]
    root_tile[...] = root.astype(jnp.bfloat16)
    pl.semaphore_wait(known, 2)

    @pl.when(l == 0)
    def _():
        roots[0] = root_tile[...]

    @pl.when(l != 0)
    def _():
        remote(root_tile, roots.at[0], ROOT, (lax.rem(o + l, owners), l)).start()

    @pl.loop(1, rounds, unroll=True)
    def _(i):
        remote(root_tile, roots.at[i], ROOT, (lax.rem(o + l + locals_ * i, owners), l)).start()

    @pl.when(jnp.logical_not(middle & rising))
    def _():
        pass_up()

    @pl.when(jnp.logical_not(middle & jnp.logical_not(rising)))
    def _():
        pass_down()

    @pl.loop(1, locals_, unroll=True)
    def _(d):
        peer = (o, lax.rem(l + d, locals_))
        mine = tops.at[pl.ds(l, 1)]
        remote(mine, mine, TOPS, peer).start()
        block = topw.at[pl.ds(l, 1)]
        remote(block, block, TOPW, peer).start()

    def to_scalars(rows, sem):
        copy = pltpu.make_async_copy(req.at[rows], req_s.at[rows], sem)
        copy.start()
        return copy

    received(req.at[pl.ds(0, near_rows - 2 * PLANE - 1)], REST)
    near_asked = to_scalars(pl.ds(0, near_rows), smem_sem.at[1])
    received(skel.at[pl.ds(0, clusters * (locals_ - 1))], SKEL)
    near_asked.wait()

    def chosen(n):
        a = skel[req_s[n, 0, o]].astype(jnp.float32)
        b = skel[req_s[n, 0, HALF + o]].astype(jnp.float32)
        return jnp.where(low, a, b).astype(jnp.bfloat16).reshape(1, NV, WIDE)

    def choose(begin, end):
        @pl.loop(begin, end, unroll=True)
        def _(n):
            far_send[pl.ds(n, 1), :, :] = chosen(n)

    def answer(n, asker):
        remote(far_send.at[pl.ds(n, 1)], far_recv.at[pl.ds(o, 1)], FARS, (asker, l)).start()

    choose(0, near_rows)

    @pl.loop(0, own_row, unroll=True)
    def _(n):
        answer(n, beside(n))

    @pl.loop(own_row + 1, near_rows, unroll=True)
    def _(n):
        answer(n, beside(n))

    members = clusters * locals_
    skel_rows[...] = skel[...].astype(jnp.float32).reshape(members * NV, WIDE).astype(jnp.bfloat16)
    column = lax.broadcasted_iota(jnp.int32, (1, NV, members * NV), 2)
    row = lax.broadcasted_iota(jnp.int32, (1, NV, members * NV), 1)
    member_of = jnp.where(lax.rem(column, NV) == row, column // NV, -1).astype(jnp.float32)
    received(req.at[pl.ds(0, below_rows + above_rows)], PASSED)
    passed = req[near_rows:owners].astype(jnp.float32)
    at = lax.broadcasted_iota(jnp.int32, passed.shape, 2)
    ones = [
        (jnp.sum(jnp.where(at == o + half, passed, 0.0), axis=2, keepdims=True) == member_of).astype(jnp.float32)
        for half in (0, HALF)
    ]
    rows = (owners - near_rows) * NV
    both = jnp.concatenate([one.reshape(rows, members * NV) for one in ones], axis=0).astype(jnp.bfloat16)
    both = dot(both, skel_rows[...])
    wide_low = lax.broadcasted_iota(jnp.int32, (rows, WIDE), 1) < HALF
    both = jnp.where(wide_low, both[:rows], both[rows:])
    far_send[near_rows:owners] = both.reshape(owners - near_rows, NV, WIDE).astype(jnp.bfloat16)

    def answer_below():
        @pl.loop(0, below_rows, unroll=True)
        def _(i):
            j = below_rows - 1 - i
            answer(near_rows + j, owner_at(-reach - 1 - j // PLANE, lax.rem(j, PLANE)))

    def answer_above():
        @pl.loop(0, above_rows, unroll=True)
        def _(i):
            j = above_rows - 1 - i
            answer(near_rows + below_rows + j, owner_at(reach + 1 + j // PLANE, lax.rem(j, PLANE)))

    above_first = (z > 2 * reach) & (z < 3 * reach)

    if above_rows:

        @pl.when(above_first)
        def _():
            answer_above()

    answer_below()

    if above_rows:

        @pl.when(jnp.logical_not(above_first))
        def _():
            answer_above()

    far_recv[pl.ds(o, 1), :, :] = far_send[pl.ds(own_row, 1), :, :]

    received(tops.at[pl.ds(0, locals_ - 1)], TOPS)
    tops_copy = pltpu.make_async_copy(tops, tops_s, smem_sem.at[2])
    tops_copy.start()
    received(topw.at[pl.ds(0, locals_ - 1)], TOPW)
    tops_copy.wait()

    @pl.when(l == 0)
    def _():
        received(roots.at[pl.ds(0, rounds - 1)], ROOT)

    @pl.when(l != 0)
    def _():
        received(roots, ROOT)

    def coupled(s):
        away = lax.rem(o - l - tops_s[s // 2, 0, s % 2] + 2 * owners, owners)
        tile = roots[away // locals_].astype(jnp.float32)
        return jnp.where(lax.rem(away, locals_) == 0, tile, 0.0)

    total_share = jnp.zeros((NV, WIDE), jnp.float32)
    for other in range(locals_):
        lhs = jnp.where(low, coupled(2 * other), coupled(2 * other + 1)).astype(jnp.bfloat16)
        block = topw[other]
        total_share = total_share + dot_t(lhs, jnp.concatenate([block, block], axis=0))
    share[pl.ds(l, 1), :, :] = total_share.reshape(1, NV, WIDE)

    @pl.loop(1, locals_, unroll=True)
    def _(d):
        mine = share.at[pl.ds(l, 1)]
        remote(mine, mine, SHARE, (o, lax.rem(l + d, locals_))).start()

    received(halo.at[0], HALO)
    received(halo.at[1], HALO2)

    def spread(pair, at):
        pair = pair.astype(jnp.float32)
        turned = pltpu.roll(pair, HALF, 1)
        ext[at] = jnp.where(low, pair, turned)
        ext[at + 1] = jnp.where(low, turned, pair)

    for q in range(REACH // 2):
        spread(halo[0, :, q * WIDE : (q + 1) * WIDE], 2 * q)
        spread(halo[1, :, q * WIDE : (q + 1) * WIDE], REACH + leaves + 2 * q)
    @pl.loop(0, pairs, unroll=4)
    def _(q):
        spread(vec_b[:, pl.ds(pl.multiple_of(q * WIDE, WIDE), WIDE)], REACH + 2 * q)

    load_src.wait()
    load_near.wait()
    zero = jnp.zeros((NV, WIDE), jnp.float32)

    def quad(pieces):
        rows = [
            jnp.concatenate([jnp.where(low, pieces[0], 0.0), zero], axis=1),
            jnp.concatenate([jnp.where(low, 0.0, pieces[1]), zero], axis=1),
            jnp.concatenate([zero, jnp.where(low, pieces[2], 0.0)], axis=1),
            jnp.concatenate([zero, jnp.where(low, 0.0, pieces[3])], axis=1),
        ]
        return jnp.concatenate(rows, axis=0).astype(jnp.bfloat16)

    offset = REACH - me * leaves

    def inside(at):
        return jnp.minimum(jnp.maximum(at, 0), leaves + 2 * REACH - 1)

    @pl.loop(0, clusters)
    def _(t):
        acc = jnp.zeros((CLUSTER_LEAVES * NV, LEAF), jnp.float32)
        for i in range(near_slots):
            lhs = quad([ext[inside(near_src[i, CLUSTER_LEAVES * t + c] + offset)] for c in range(CLUSTER_LEAVES)])
            acc = acc + dot_t(lhs, near_b[i, :, pl.ds(pl.multiple_of(t * QUAD, QUAD), QUAD)])
        for c in range(0, CLUSTER_LEAVES, 2):
            near_res[2 * t + c // 2] = jnp.concatenate(
                [acc[c * NV : (c + 1) * NV], acc[(c + 1) * NV : (c + 2) * NV]], axis=1
            )

    received(share.at[pl.ds(0, locals_ - 1)], SHARE)
    summed = share[0]
    for other in range(1, locals_):
        summed = summed + share[other]
    root_out = summed[:, 0:RANK].astype(jnp.bfloat16)
    downward = dot(root_out, root_b[...])
    rank_copy.wait()
    load_owner_s.wait()
    load_count.wait()
    load_far.wait()

    received(far_recv.at[pl.ds(0, owners - 1)], FARS)

    def picked(t, f):
        source = owner_s[t, f]
        tile = far_recv[source].astype(jnp.float32)
        tile = jnp.where(rank_s[t, source] == t % 2, tile, pltpu.roll(tile, HALF, 1))
        return jnp.where(f < count_s[t], tile, 0.0)

    for g in range(clusters // 4):
        acc = jnp.zeros((4 * NV, RANK), jnp.float32)
        for f in range(slots):
            lhs = quad([picked(4 * g + t, f) for t in range(4)])
            acc = acc + dot_t(lhs, far_b[f, :, g * QUAD : (g + 1) * QUAD])
        for t in range(4):
            at = 4 * g + t
            cluster_out = acc[t * NV : (t + 1) * NV] + downward[:, at * RANK : (at + 1) * RANK]
            leaf_out = dot(cluster_out.astype(jnp.bfloat16), up_b[:, at * QUAD : (at + 1) * QUAD]).astype(jnp.bfloat16)
            for c in range(2):
                q = 2 * at + c
                result = dot(leaf_out[:, c * WIDE : (c + 1) * WIDE], pair_basis[q]) + near_res[q]
                out[:, q * WIDE : (q + 1) * WIDE] = result.astype(jnp.bfloat16)

    sent(skel.at[pl.ds(0, clusters * (locals_ - 1))], SKEL)
    sent(part.at[pl.ds(0, locals_ - 1)], PART)
    sent(req.at[pl.ds(0, near_rows - 1)], REST)
    sent(req.at[pl.ds(0, below_rows + above_rows)], PASSED)
    sent(tops.at[pl.ds(0, locals_ - 1)], TOPS)
    sent(topw.at[pl.ds(0, locals_ - 1)], TOPW)
    sent(halo.at[0], HALO)
    sent(halo.at[1], HALO2)

    @pl.when(l == 0)
    def _():
        sent(roots.at[pl.ds(0, rounds - 1)], ROOT)

    @pl.when(l != 0)
    def _():
        sent(roots, ROOT)

    sent(share.at[pl.ds(0, locals_ - 1)], SHARE)
    sent(far_recv.at[pl.ds(0, owners - 1)], FARS)


def per_device(
    owners,
    locals_,
    vectors,
    leaf_basis,
    near_blocks,
    near_source,
    up_transfer,
    far_owner,
    far_member,
    far_count,
    far_blocks,
    root_transfer,
    top_source,
    top_blocks,
):
    clusters = far_owner.shape[0]
    leaves = clusters * CLUSTER_LEAVES
    bf16, f32, i32 = jnp.bfloat16, jnp.float32, jnp.int32
    hbm = pl.BlockSpec(memory_space=pltpu.HBM)
    vmem = pl.BlockSpec(memory_space=pltpu.VMEM)
    big = (vectors, leaf_basis, near_blocks, up_transfer, far_blocks, root_transfer, top_blocks)
    return pl.pallas_call(
        functools.partial(kernel, owners, locals_),
        out_shape=pltpu.VMEM(vectors.shape, bf16),
        in_specs=[hbm] * 12,
        out_specs=vmem,
        scratch_shapes=[pltpu.VMEM(a.shape, bf16) for a in big]
        + [
            pltpu.SMEM((near_source.shape[1], near_source.shape[0]), i32),
            pltpu.SMEM(far_owner.shape, i32),
            pltpu.SMEM(far_count.shape, i32),
            pltpu.VMEM(far_owner.shape, i32),
            pltpu.VMEM(far_owner.shape, i32),
            pltpu.VMEM(top_source.shape, i32),
            pltpu.SemaphoreType.DMA((13,)),
            pltpu.VMEM((leaves // 2, WIDE, WIDE), bf16),
            pltpu.VMEM((leaves + 2 * REACH, NV, WIDE), f32),
            pltpu.VMEM((leaves // 2, NV, WIDE), f32),
            pltpu.VMEM((clusters, WIDE), i32),
            pltpu.SMEM((clusters, WIDE), i32),
            pltpu.VMEM((2, NV, REACH * LEAF), bf16),
            pltpu.VMEM((owners, 1, WIDE), i32),
            pltpu.SMEM((owners, 1, WIDE), i32),
            pltpu.VMEM((1, WIDE), i32),
            pltpu.VMEM((locals_, 1, WIDE), i32),
            pltpu.SMEM((locals_, 1, WIDE), i32),
            pltpu.VMEM((locals_, RANK, WIDE), bf16),
            pltpu.VMEM((clusters * locals_, NV, WIDE), bf16),
            pltpu.VMEM((clusters * locals_ * NV, WIDE), bf16),
            pltpu.VMEM((locals_, NV, WIDE), f32),
            pltpu.VMEM((NV, WIDE), bf16),
            pltpu.VMEM((owners // locals_, NV, WIDE), bf16),
            pltpu.VMEM((owners, NV, WIDE), bf16),
            pltpu.VMEM((owners, NV, WIDE), bf16),
            pltpu.VMEM((locals_, NV, WIDE), f32),
            pltpu.SemaphoreType.DMA((3,)),
            pltpu.SemaphoreType.DMA((KINDS,)),
            pltpu.SemaphoreType.DMA((KINDS,)),
            pltpu.SemaphoreType.REGULAR,
        ],
        compiler_params=pltpu.CompilerParams(
            collective_id=0, has_side_effects=True, vmem_limit_bytes=32 * 1024 * 1024
        ),
    )(*[pltpu.with_memory_space_constraint(a, pltpu.HBM) for a in (*big, near_source.T, far_owner, far_member, far_count, top_source)])


def solution(mesh):
    return jax.shard_map(
        functools.partial(per_device, mesh.shape["owner"], mesh.shape["local"]),
        mesh=mesh,
        in_specs=(
            P(None, ("owner", "local")),
            P(None, ("owner", "local")),
            P(None, None, ("owner", "local")),
            P(("owner", "local"), None),
            P(None, ("owner", "local")),
            P(("owner", "local"), None),
            P(("owner", "local"), None),
            P(("owner", "local")),
            P(None, None, ("owner", "local")),
            P(None, ("owner", "local")),
            P("owner", "local"),
            P("local", None, "owner"),
        ),
        out_specs=P(None, ("owner", "local")),
        check_vma=False,
    )
```

```python
import functools

import jax
import jax.numpy as jnp
from jax import lax
from jax.experimental import pallas as pl
from jax.experimental.pallas import tpu as pltpu
from jax.sharding import PartitionSpec as P

MESH = pl.DeviceIdType.MESH
KINDS = 14
NV = 8
LEAF = 64
RANK = 64
CLUSTER_LEAVES = 4
REACH = 4
HALF = 64
PLANE = 4
WIDE = 128
QUAD = 256


def dot(left, right):
    return jnp.dot(left, right, preferred_element_type=jnp.float32)


def dot_t(left, right):
    return lax.dot_general(left, right, (((1,), (1,)), ((), ())), preferred_element_type=jnp.float32)


def wait_bytes(ref, sem):
    pltpu.make_async_copy(ref, ref, sem).wait()


def kernel(
    owners,
    locals_,
    vec,
    basis,
    near,
    up,
    far,
    root_t,
    top_b,
    near_src_h,
    owner_h,
    member_h,
    count_h,
    top_src_h,
    out,
    vec_b,
    basis_b,
    near_b,
    up_b,
    far_b,
    root_b,
    topb_b,
    near_src,
    owner_s,
    count_s,
    owner_v,
    member_v,
    top_src,
    load_sem,
    pair_basis,
    ext,
    near_res,
    rank_b,
    rank_s,
    halo,
    req,
    req_s,
    tops_row,
    tops,
    tops_s,
    topw,
    skel,
    skel_rows,
    part,
    root_tile,
    roots,
    far_send,
    far_recv,
    share,
    smem_sem,
    send_sem,
    recv_sem,
    known,
):
    o, l = lax.axis_index("owner"), lax.axis_index("local")
    me = o * locals_ + l
    total = owners * locals_
    clusters = skel.shape[0] // locals_
    slots = far_b.shape[0]
    near_slots = near_b.shape[0]
    leaves = clusters * CLUSTER_LEAVES
    pairs = leaves // 2
    rounds = owners // locals_
    left, right = lax.rem(me + total - 1, total), lax.rem(me + 1, total)
    left_id = (left // locals_, lax.rem(left, locals_))
    right_id = (right // locals_, lax.rem(right, locals_))
    HALO, HALO2, REST, FROM_LOW, FROM_HIGH, PASSED, TOPS, TOPW, SKEL, PART, ROOT, FARS, SHARE, PASSED_DOWN = range(KINDS)
    depth = owners // PLANE
    reach = depth // 4
    z, y = o // PLANE, lax.rem(o, PLANE)
    own_row = reach * PLANE
    top_rows = 2 * reach * PLANE
    near_rows = (2 * reach + 1) * PLANE
    below_rows = reach * PLANE
    above_rows = (reach - 1) * PLANE

    def owner_at(dz, dy):
        return lax.rem(z + dz + depth, depth) * PLANE + lax.rem(y + dy, PLANE)

    def beside(n):
        return owner_at(n // PLANE - reach, lax.rem(n, PLANE))


    def remote(source, target, kind, device):
        return pltpu.make_async_remote_copy(
            src_ref=source,
            dst_ref=target,
            send_sem=send_sem.at[REST if kind in (FROM_LOW, FROM_HIGH) else kind],
            recv_sem=recv_sem.at[kind],
            device_id=device,
            device_id_type=MESH,
        )

    def received(ref, kind):
        wait_bytes(ref, recv_sem.at[kind])

    def sent(ref, kind):
        wait_bytes(ref, send_sem.at[kind])

    def load(i, source, target):
        copy = pltpu.make_async_copy(source, target, load_sem.at[i])
        copy.start()
        return copy

    load_vec = load(2, vec, vec_b)
    load_basis = load(3, basis, basis_b)
    load_up = load(4, up, up_b)

    barrier = pltpu.get_barrier_semaphore()

    def greet(device):
        pl.semaphore_signal(barrier, inc=1, device_id=device, device_id_type=MESH)

    def greet_planes(begin, end):
        @pl.loop(begin, end, unroll=True)
        def _(n):
            greet((beside(n), l))

    greet_planes(0, PLANE)
    greet_planes(top_rows, near_rows)
    greet_planes(PLANE, own_row)
    greet_planes(own_row + 1, top_rows)

    @pl.loop(1, locals_, unroll=True)
    def _(d):
        greet((o, lax.rem(l + d, locals_)))

    greet(left_id)
    greet(right_id)

    load_owner = load(0, owner_h, owner_v)
    load_member = load(1, member_h, member_v)
    load_root = load(5, root_t, root_b)
    load_top = load(6, top_src_h, top_src)
    load_topb = load(7, top_b, topb_b)
    load_src = load(8, near_src_h, near_src)
    load_near = load(9, near, near_b)
    load_owner_s = load(10, owner_h, owner_s)
    load_count = load(11, count_h, count_s)
    load_far = load(12, far, far_b)

    lane = lax.broadcasted_iota(jnp.int32, (1, WIDE), 1)
    lanes = lax.broadcasted_iota(jnp.int32, (clusters, WIDE), 1)
    key = jnp.where(lanes >= HALF, lanes - HALF, lanes)
    named = jnp.zeros((clusters, WIDE), jnp.int32)
    member = jnp.zeros((clusters, WIDE), jnp.int32)
    load_owner.wait()
    load_member.wait()
    for f in range(slots):
        same = owner_v[:, f : f + 1] == key
        named = jnp.where(same, 1, named)
        member = jnp.where(same, member_v[:, f : f + 1], member)
    second = (lane >= HALF).astype(jnp.int32)
    run = jnp.zeros((1, WIDE), jnp.int32)
    wanted = jnp.zeros((1, WIDE), jnp.int32)
    for t in range(clusters):
        rank_b[t : t + 1, :] = run
        wanted = jnp.where(run == second, wanted + member[t : t + 1], wanted)
        run = run + named[t : t + 1]
    req[own_row] = wanted
    rank_copy = pltpu.make_async_copy(rank_b, rank_s, smem_sem.at[0])
    rank_copy.start()
    tops_row[...] = jnp.zeros((1, WIDE), jnp.int32)
    load_top.wait()
    tops_row[:, 0:2] = top_src[...]
    tops[pl.ds(l, 1), :, :] = tops_row[...].reshape(1, 1, WIDE)

    low = lax.broadcasted_iota(jnp.int32, (NV, WIDE), 1) < HALF
    low_ones = (lax.broadcasted_iota(jnp.int32, (RANK, WIDE), 1) < HALF).astype(jnp.bfloat16)
    high_ones = (lax.broadcasted_iota(jnp.int32, (RANK, WIDE), 1) >= HALF).astype(jnp.bfloat16)
    load_vec.wait()
    load_basis.wait()
    load_up.wait()
    first = l * clusters

    @pl.loop(0, clusters)
    def _(t):
        parts = []
        for c in range(2):
            q = 2 * t + c
            lanes_q = pl.ds(pl.multiple_of(q * WIDE, WIDE), WIDE)
            block = basis_b[:, lanes_q]
            diagonal = jnp.concatenate([block * low_ones, block * high_ones], axis=0)
            pair_basis[q] = diagonal
            parts.append(dot_t(vec_b[:, lanes_q], diagonal))
        leaf_skel = jnp.concatenate(parts, axis=1).astype(jnp.bfloat16)
        block = up_b[:, pl.ds(pl.multiple_of(t * QUAD, QUAD), QUAD)]
        tile = dot_t(leaf_skel, jnp.concatenate([block, block], axis=0)).astype(jnp.bfloat16)
        skel[pl.ds(first + t, 1), :, :] = tile.reshape(1, NV, WIDE)

    tiles = [skel[first + t].astype(jnp.float32) for t in range(clusters)]
    load_root.wait()
    rows = jnp.concatenate(
        [jnp.where(low, tiles[2 * q], tiles[2 * q + 1]) for q in range(clusters // 2)], axis=1
    ).astype(jnp.bfloat16)
    rootward = root_b[...]
    part[pl.ds(l, 1), :, :] = dot_t(rows, jnp.concatenate([rootward, rootward], axis=0)).reshape(1, NV, WIDE)

    load_topb.wait()
    topw[pl.ds(l, 1), :, :] = jnp.concatenate([topb_b[0], topb_b[1]], axis=1).reshape(1, RANK, WIDE)

    pl.semaphore_wait(barrier, near_rows - 1 + locals_ - 1 + 2)

    def share_skeletons():
        @pl.loop(1, locals_, unroll=True)
        def _(d):
            mine = part.at[pl.ds(l, 1)]
            remote(mine, mine, PART, (o, lax.rem(l + d, locals_))).start()

        @pl.loop(1, locals_, unroll=True)
        def _(d):
            own = skel.at[pl.ds(first, clusters)]
            remote(own, own, SKEL, (o, lax.rem(l + d, locals_))).start()

    def ask(begin, end, kind):
        @pl.loop(begin, end, unroll=True)
        def _(n):
            row = (2 * reach - n // PLANE) * PLANE + lax.rem(PLANE - lax.rem(n, PLANE), PLANE)
            remote(req.at[own_row], req.at[row], kind, (beside(n), l)).start()

    def pass_up():
        received(req.at[pl.ds(0, PLANE)], FROM_LOW)

        @pl.loop(0, reach, unroll=True)
        def _(k):
            rows = pl.ds(near_rows + k * PLANE, PLANE)
            remote(req.at[pl.ds(0, PLANE)], req.at[rows], PASSED, (owner_at(k + 1, 0), l)).start()

    def pass_down():
        received(req.at[pl.ds(top_rows, PLANE)], FROM_HIGH)

        @pl.loop(0, reach - 1, unroll=True)
        def _(k):
            rows = pl.ds(near_rows + below_rows + k * PLANE, PLANE)
            remote(req.at[pl.ds(top_rows, PLANE)], req.at[rows], PASSED_DOWN, (owner_at(-k - 1, 0), l)).start()

    away = jnp.minimum(z, depth - z)
    late = away * 4 >= depth + 2 * reach
    middle = (away + 1 >= reach) & (away <= reach + 1)
    rising = z < 2 * reach

    @pl.when(late)
    def _():
        share_skeletons()

    ask(top_rows, near_rows, FROM_LOW)
    ask(0, PLANE, FROM_HIGH)
    for dz in (-reach, reach):
        pl.semaphore_signal(known, inc=1, device_id=(owner_at(dz, 0), l), device_id_type=MESH)

    @pl.when(jnp.logical_not(late))
    def _():
        share_skeletons()

    ask(PLANE, own_row, REST)
    ask(own_row + 1, top_rows, REST)

    @pl.loop(1, locals_, unroll=True)
    def _(d):
        peer = (o, lax.rem(l + d, locals_))
        mine = tops.at[pl.ds(l, 1)]
        remote(mine, mine, TOPS, peer).start()
        block = topw.at[pl.ds(l, 1)]
        remote(block, block, TOPW, peer).start()

    edge = REACH * LEAF
    width = leaves * LEAF
    remote(vec_b.at[:, pl.ds(width - edge, edge)], halo.at[0], HALO, right_id).start()
    remote(vec_b.at[:, pl.ds(0, edge)], halo.at[1], HALO2, left_id).start()

    @pl.when(middle & rising)
    def _():
        pass_up()

    @pl.when(middle & jnp.logical_not(rising))
    def _():
        pass_down()

    received(part.at[pl.ds(0, locals_ - 1)], PART)
    root = part[0]
    for other in range(1, locals_):
        root = root + part[other]
    root_tile[...] = root.astype(jnp.bfloat16)
    pl.semaphore_wait(known, 2)

    @pl.when(l == 0)
    def _():
        roots[0] = root_tile[...]

    @pl.when(l != 0)
    def _():
        remote(root_tile, roots.at[0], ROOT, (lax.rem(o + l, owners), l)).start()

    @pl.loop(1, rounds, unroll=True)
    def _(i):
        remote(root_tile, roots.at[i], ROOT, (lax.rem(o + l + locals_ * i, owners), l)).start()

    @pl.when(jnp.logical_not(middle & rising))
    def _():
        pass_up()

    @pl.when(jnp.logical_not(middle & jnp.logical_not(rising)))
    def _():
        pass_down()

    def to_scalars(rows, sem):
        copy = pltpu.make_async_copy(req.at[rows], req_s.at[rows], sem)
        copy.start()
        return copy

    received(req.at[pl.ds(0, near_rows - 2 * PLANE - 1)], REST)
    near_asked = to_scalars(pl.ds(0, near_rows), smem_sem.at[1])
    received(skel.at[pl.ds(0, clusters * (locals_ - 1))], SKEL)
    near_asked.wait()

    def chosen(n):
        a = skel[req_s[n, 0, o]].astype(jnp.float32)
        b = skel[req_s[n, 0, HALF + o]].astype(jnp.float32)
        return jnp.where(low, a, b).astype(jnp.bfloat16).reshape(1, NV, WIDE)

    def choose(begin, end):
        @pl.loop(begin, end, unroll=True)
        def _(n):
            far_send[pl.ds(n, 1), :, :] = chosen(n)

    def answer(n, asker):
        remote(far_send.at[pl.ds(n, 1)], far_recv.at[pl.ds(o, 1)], FARS, (asker, l)).start()

    choose(0, near_rows)

    @pl.loop(0, own_row, unroll=True)
    def _(n):
        answer(n, beside(n))

    @pl.loop(own_row + 1, near_rows, unroll=True)
    def _(n):
        answer(n, beside(n))

    members = clusters * locals_
    skel_rows[...] = skel[...].astype(jnp.float32).reshape(members * NV, WIDE).astype(jnp.bfloat16)
    column = lax.broadcasted_iota(jnp.int32, (1, NV, members * NV), 2)
    row = lax.broadcasted_iota(jnp.int32, (1, NV, members * NV), 1)
    member_of = jnp.where(lax.rem(column, NV) == row, column // NV, -1).astype(jnp.float32)

    def choose_passed(begin, count, kind):
        received(req.at[pl.ds(0, count)], kind)
        passed = req[begin : begin + count].astype(jnp.float32)
        at = lax.broadcasted_iota(jnp.int32, passed.shape, 2)
        ones = [
            (jnp.sum(jnp.where(at == o + half, passed, 0.0), axis=2, keepdims=True) == member_of).astype(jnp.float32)
            for half in (0, HALF)
        ]
        rows = count * NV
        both = jnp.concatenate([one.reshape(rows, members * NV) for one in ones], axis=0).astype(jnp.bfloat16)
        both = dot(both, skel_rows[...])
        wide_low = lax.broadcasted_iota(jnp.int32, (rows, WIDE), 1) < HALF
        both = jnp.where(wide_low, both[:rows], both[rows:])
        far_send[begin : begin + count] = both.reshape(count, NV, WIDE).astype(jnp.bfloat16)

    def answer_below():
        choose_passed(near_rows, below_rows, PASSED)

        @pl.loop(0, below_rows, unroll=True)
        def _(i):
            j = below_rows - 1 - i
            answer(near_rows + j, owner_at(-reach - 1 - j // PLANE, lax.rem(j, PLANE)))

    def answer_above():
        choose_passed(near_rows + below_rows, above_rows, PASSED_DOWN)

        @pl.loop(0, above_rows, unroll=True)
        def _(i):
            j = above_rows - 1 - i
            answer(near_rows + below_rows + j, owner_at(reach + 1 + j // PLANE, lax.rem(j, PLANE)))

    above_first = (z > 2 * reach) & (z < 3 * reach)

    if above_rows:

        @pl.when(above_first)
        def _():
            answer_above()

    answer_below()

    if above_rows:

        @pl.when(jnp.logical_not(above_first))
        def _():
            answer_above()

    far_recv[pl.ds(o, 1), :, :] = far_send[pl.ds(own_row, 1), :, :]

    received(tops.at[pl.ds(0, locals_ - 1)], TOPS)
    tops_copy = pltpu.make_async_copy(tops, tops_s, smem_sem.at[2])
    tops_copy.start()
    received(topw.at[pl.ds(0, locals_ - 1)], TOPW)
    tops_copy.wait()

    @pl.when(l == 0)
    def _():
        received(roots.at[pl.ds(0, rounds - 1)], ROOT)

    @pl.when(l != 0)
    def _():
        received(roots, ROOT)

    def coupled(s):
        away = lax.rem(o - l - tops_s[s // 2, 0, s % 2] + 2 * owners, owners)
        tile = roots[away // locals_].astype(jnp.float32)
        return jnp.where(lax.rem(away, locals_) == 0, tile, 0.0)

    total_share = jnp.zeros((NV, WIDE), jnp.float32)
    for other in range(locals_):
        lhs = jnp.where(low, coupled(2 * other), coupled(2 * other + 1)).astype(jnp.bfloat16)
        block = topw[other]
        total_share = total_share + dot_t(lhs, jnp.concatenate([block, block], axis=0))
    share[pl.ds(l, 1), :, :] = total_share.reshape(1, NV, WIDE)

    @pl.loop(1, locals_, unroll=True)
    def _(d):
        mine = share.at[pl.ds(l, 1)]
        remote(mine, mine, SHARE, (o, lax.rem(l + d, locals_))).start()

    received(halo.at[0], HALO)
    received(halo.at[1], HALO2)

    def spread(pair, at):
        pair = pair.astype(jnp.float32)
        turned = pltpu.roll(pair, HALF, 1)
        ext[at] = jnp.where(low, pair, turned)
        ext[at + 1] = jnp.where(low, turned, pair)

    for q in range(REACH // 2):
        spread(halo[0, :, q * WIDE : (q + 1) * WIDE], 2 * q)
        spread(halo[1, :, q * WIDE : (q + 1) * WIDE], REACH + leaves + 2 * q)
    @pl.loop(0, pairs, unroll=4)
    def _(q):
        spread(vec_b[:, pl.ds(pl.multiple_of(q * WIDE, WIDE), WIDE)], REACH + 2 * q)

    load_src.wait()
    load_near.wait()
    zero = jnp.zeros((NV, WIDE), jnp.float32)

    def quad(pieces):
        rows = [
            jnp.concatenate([jnp.where(low, pieces[0], 0.0), zero], axis=1),
            jnp.concatenate([jnp.where(low, 0.0, pieces[1]), zero], axis=1),
            jnp.concatenate([zero, jnp.where(low, pieces[2], 0.0)], axis=1),
            jnp.concatenate([zero, jnp.where(low, 0.0, pieces[3])], axis=1),
        ]
        return jnp.concatenate(rows, axis=0).astype(jnp.bfloat16)

    offset = REACH - me * leaves

    def inside(at):
        return jnp.minimum(jnp.maximum(at, 0), leaves + 2 * REACH - 1)

    @pl.loop(0, clusters)
    def _(t):
        acc = jnp.zeros((CLUSTER_LEAVES * NV, LEAF), jnp.float32)
        for i in range(near_slots):
            lhs = quad([ext[inside(near_src[i, CLUSTER_LEAVES * t + c] + offset)] for c in range(CLUSTER_LEAVES)])
            acc = acc + dot_t(lhs, near_b[i, :, pl.ds(pl.multiple_of(t * QUAD, QUAD), QUAD)])
        for c in range(0, CLUSTER_LEAVES, 2):
            near_res[2 * t + c // 2] = jnp.concatenate(
                [acc[c * NV : (c + 1) * NV], acc[(c + 1) * NV : (c + 2) * NV]], axis=1
            )

    received(share.at[pl.ds(0, locals_ - 1)], SHARE)
    summed = share[0]
    for other in range(1, locals_):
        summed = summed + share[other]
    root_out = summed[:, 0:RANK].astype(jnp.bfloat16)
    downward = dot(root_out, root_b[...])
    rank_copy.wait()
    load_owner_s.wait()
    load_count.wait()
    load_far.wait()

    received(far_recv.at[pl.ds(0, owners - 1)], FARS)

    def picked(t, f):
        source = owner_s[t, f]
        tile = far_recv[source].astype(jnp.float32)
        tile = jnp.where(rank_s[t, source] == t % 2, tile, pltpu.roll(tile, HALF, 1))
        return jnp.where(f < count_s[t], tile, 0.0)

    for g in range(clusters // 4):
        lhs = jnp.concatenate([quad([picked(4 * g + t, f) for t in range(4)]) for f in range(slots)], axis=1)
        rhs = jnp.concatenate([far_b[f, :, g * QUAD : (g + 1) * QUAD] for f in range(slots)], axis=1)
        acc = dot_t(lhs, rhs)
        for t in range(4):
            at = 4 * g + t
            cluster_out = acc[t * NV : (t + 1) * NV] + downward[:, at * RANK : (at + 1) * RANK]
            leaf_out = dot(cluster_out.astype(jnp.bfloat16), up_b[:, at * QUAD : (at + 1) * QUAD]).astype(jnp.bfloat16)
            for c in range(2):
                q = 2 * at + c
                result = dot(leaf_out[:, c * WIDE : (c + 1) * WIDE], pair_basis[q]) + near_res[q]
                out[:, q * WIDE : (q + 1) * WIDE] = result.astype(jnp.bfloat16)

    sent(skel.at[pl.ds(0, clusters * (locals_ - 1))], SKEL)
    sent(part.at[pl.ds(0, locals_ - 1)], PART)
    sent(req.at[pl.ds(0, near_rows - 1)], REST)
    sent(req.at[pl.ds(0, below_rows)], PASSED)
    if above_rows:
        sent(req.at[pl.ds(0, above_rows)], PASSED_DOWN)
    sent(tops.at[pl.ds(0, locals_ - 1)], TOPS)
    sent(topw.at[pl.ds(0, locals_ - 1)], TOPW)
    sent(halo.at[0], HALO)
    sent(halo.at[1], HALO2)

    @pl.when(l == 0)
    def _():
        sent(roots.at[pl.ds(0, rounds - 1)], ROOT)

    @pl.when(l != 0)
    def _():
        sent(roots, ROOT)

    sent(share.at[pl.ds(0, locals_ - 1)], SHARE)
    sent(far_recv.at[pl.ds(0, owners - 1)], FARS)


def per_device(
    owners,
    locals_,
    vectors,
    leaf_basis,
    near_blocks,
    near_source,
    up_transfer,
    far_owner,
    far_member,
    far_count,
    far_blocks,
    root_transfer,
    top_source,
    top_blocks,
):
    clusters = far_owner.shape[0]
    leaves = clusters * CLUSTER_LEAVES
    bf16, f32, i32 = jnp.bfloat16, jnp.float32, jnp.int32
    hbm = pl.BlockSpec(memory_space=pltpu.HBM)
    vmem = pl.BlockSpec(memory_space=pltpu.VMEM)
    big = (vectors, leaf_basis, near_blocks, up_transfer, far_blocks, root_transfer, top_blocks)
    return pl.pallas_call(
        functools.partial(kernel, owners, locals_),
        out_shape=pltpu.VMEM(vectors.shape, bf16),
        in_specs=[hbm] * 12,
        out_specs=vmem,
        scratch_shapes=[pltpu.VMEM(a.shape, bf16) for a in big]
        + [
            pltpu.SMEM((near_source.shape[1], near_source.shape[0]), i32),
            pltpu.SMEM(far_owner.shape, i32),
            pltpu.SMEM(far_count.shape, i32),
            pltpu.VMEM(far_owner.shape, i32),
            pltpu.VMEM(far_owner.shape, i32),
            pltpu.VMEM(top_source.shape, i32),
            pltpu.SemaphoreType.DMA((13,)),
            pltpu.VMEM((leaves // 2, WIDE, WIDE), bf16),
            pltpu.VMEM((leaves + 2 * REACH, NV, WIDE), f32),
            pltpu.VMEM((leaves // 2, NV, WIDE), f32),
            pltpu.VMEM((clusters, WIDE), i32),
            pltpu.SMEM((clusters, WIDE), i32),
            pltpu.VMEM((2, NV, REACH * LEAF), bf16),
            pltpu.VMEM((owners, 1, WIDE), i32),
            pltpu.SMEM((owners, 1, WIDE), i32),
            pltpu.VMEM((1, WIDE), i32),
            pltpu.VMEM((locals_, 1, WIDE), i32),
            pltpu.SMEM((locals_, 1, WIDE), i32),
            pltpu.VMEM((locals_, RANK, WIDE), bf16),
            pltpu.VMEM((clusters * locals_, NV, WIDE), bf16),
            pltpu.VMEM((clusters * locals_ * NV, WIDE), bf16),
            pltpu.VMEM((locals_, NV, WIDE), f32),
            pltpu.VMEM((NV, WIDE), bf16),
            pltpu.VMEM((owners // locals_, NV, WIDE), bf16),
            pltpu.VMEM((owners, NV, WIDE), bf16),
            pltpu.VMEM((owners, NV, WIDE), bf16),
            pltpu.VMEM((locals_, NV, WIDE), f32),
            pltpu.SemaphoreType.DMA((3,)),
            pltpu.SemaphoreType.DMA((KINDS,)),
            pltpu.SemaphoreType.DMA((KINDS,)),
            pltpu.SemaphoreType.REGULAR,
        ],
        compiler_params=pltpu.CompilerParams(
            collective_id=0, has_side_effects=True, vmem_limit_bytes=32 * 1024 * 1024
        ),
    )(*[pltpu.with_memory_space_constraint(a, pltpu.HBM) for a in (*big, near_source.T, far_owner, far_member, far_count, top_source)])


def solution(mesh):
    return jax.shard_map(
        functools.partial(per_device, mesh.shape["owner"], mesh.shape["local"]),
        mesh=mesh,
        in_specs=(
            P(None, ("owner", "local")),
            P(None, ("owner", "local")),
            P(None, None, ("owner", "local")),
            P(("owner", "local"), None),
            P(None, ("owner", "local")),
            P(("owner", "local"), None),
            P(("owner", "local"), None),
            P(("owner", "local")),
            P(None, None, ("owner", "local")),
            P(None, ("owner", "local")),
            P("owner", "local"),
            P("local", None, "owner"),
        ),
        out_specs=P(None, ("owner", "local")),
        check_vma=False,
    )
```
